32 devices in a mesh: dom: 2 (over y), exp: 16 (over z, x, core).
Axes of the slice: x: 2, y: 2, z: 4, core: 2. Of those that a mesh axis runs over, the one named last changes fastest.
Arguments:
- queries: bfloat16 [128, 4096], P(('dom', 'exp')), parts along dimension 0
- new_keys: bfloat16 [128, 1024], P(('dom', 'exp')), parts along dimension 0, may hold values from -6 to 6
- new_values: bfloat16 [128, 1024], P(('dom', 'exp')), parts along dimension 0, may hold values from -6 to 6
- cache_keys: bfloat16 [128, 32, 1024], P(('dom', 'exp')), parts along dimension 0
- cache_values: bfloat16 [128, 32, 1024], P(('dom', 'exp')), parts along dimension 0, may hold values from -6 to 6
- lengths: int32 [128], P(('dom', 'exp')), parts along dimension 0, may hold values from 2 to 32, as said below
- norm_gain: float32 [4096], replicated, may hold values from 0.5 to 1.5
- route_ids: int32 [128, 2], P(('dom', 'exp')), parts along dimension 0, may hold values from 0 to 7, all different within a row; in each aligned block of 4 rows (0 to 3, 4 to 7, ...) at most 2 rows name the same one
- route_weights: float32 [128, 2], P(('dom', 'exp')), parts along dimension 0, may hold values from 0.1 to 1
- active_blocks: int32 [16, 64], P('dom'), parts along dimension 0, may hold values 0 or 1
- gate_weight: bfloat16 [65536, 4096], P('exp'), may hold values from -0.09375 to 0.09375
- up_weight: bfloat16 [65536, 4096], P('exp'), may hold values from -0.09375 to 0.09375
- down_weight: bfloat16 [65536, 4096], P('exp'), may hold values from -0.1875 to 0.1875
Outputs:
- attended: bfloat16 [128, 4096], P(('dom', 'exp')), parts along dimension 0
- expert_out: bfloat16 [128, 4096], P(('dom', 'exp')), parts along dimension 0
The draws below stay inside these ranges and needn't reach their ends.
There are 2 independent parts, one for each index of `dom`. The reference program is written for one: setup_inputs(seed, part) draws one part's arguments, and reference() takes and returns one part's arrays. A program takes and returns all parts, laid end to end along the dimension named above; an argument that names none is the same for every part. Nothing has to cross between parts.
Inputs may be any that keep to these rules, and one draw needn't show every extreme that they name: `lengths`: the first row of the group has 32 positions in use. `route_ids`: among the rows of one device no expert is named by more than 2 rows, a bound that some block reaches.
All inputs are finite; a program needn't handle non-finite values.
Results may differ from the reference program's by a relative error of at most 0.014.
Values may be sent and summed in bfloat16 or wider, within the bound.
No kernel may reach another device: no remote copies, remote signals or barrier semaphores. Data moves between devices by JAX's collectives and lax.ppermute only.
A program may use at most 192 MiB of HBM per device.

```python
import math
import jax
import jax.numpy as jnp
import numpy as np
from jax import lax

D = 4096
HEADS = 32
KV_HEADS = 8
HEAD_DIM = 128
EXPERTS = 8
FF = 8192
BLOCK = 128
ROWS_DEV = 4
CTX = 32
CAP = 2
ROWS = 64
GROUPS = 2
FF_DEV = 4096
N_EXP = 16


def draw_queries(key, part):
    key = jax.random.fold_in(key, 21)
    result = jnp.clip(jax.random.normal(key, (ROWS, HEADS * HEAD_DIM), jnp.float32), -6.0, 6.0)
    return result.astype(jnp.bfloat16)


def draw_cache_keys(key, part):
    key = jax.random.fold_in(key, 22)
    result = jnp.clip(jax.random.normal(key, (ROWS, CTX, KV_HEADS * HEAD_DIM), jnp.float32), -6.0, 6.0)
    return result.astype(jnp.bfloat16)


def draw_lengths(key, part):
    key = jax.random.fold_in(key, 23)
    drawn = jax.random.randint(key, (ROWS,), 2, CTX + 1)
    return drawn.at[0].set(CTX).astype(jnp.int32)


def touch_ends(values, rng, smallest, top_value):
    dims = values.shape
    spot = [jax.random.randint(jax.random.fold_in(rng, axis), (), 0, dims[axis]) for axis in range(len(dims))]
    values = values.at[tuple(spot)].set(smallest)
    longest = dims.index(max(dims))
    spot[longest] = (spot[longest] + 1) % dims[longest]
    return values.at[tuple(spot)].set(top_value)


def block_scale(rng, extent, cuts, least, high):
    gain, own = 1.0, jax.random.fold_in(rng, 6)
    for dim, parts in cuts:
        steps = jnp.exp(jax.random.uniform(jax.random.fold_in(own, dim), (parts,), jnp.float32, least / len(cuts), high / len(cuts)))
        gain = gain * jnp.repeat(steps, extent[dim] // parts).reshape([-1 if axis == dim else 1 for axis in range(len(extent))])
    return gain


def shared_out(key, own, number, rows, count, top, bound, lean):
    sequence = jax.random.permutation(key, count)
    packed, ordinary = shares(count, rows * top, bound, lean, True), shares(count, rows * top, bound, lean, False)
    places = jnp.arange(count)

    def named(tallies, offset_by):
        used = int((tallies > 0).sum())
        fixed = max(1, used // 4)
        moved = fixed + (places - fixed + offset_by * (used - fixed)) % max(1, count - fixed)
        return jnp.zeros((count,), jnp.int32).at[sequence[jnp.where(places < fixed, places, moved)]].set(jnp.asarray(tallies, jnp.int32))

    tallies = jnp.where(number % 4 == 0, named(packed, number // 4), named(ordinary, number - number // 4 - 1))
    mixed = jax.random.permutation(jax.random.fold_in(own, 3), count)
    giver, taker = mixed[0:count // 2 * 2:2], mixed[1:count // 2 * 2:2]
    room = jnp.minimum(tallies[giver] - 1, bound - tallies[taker]) // 2
    room = jnp.where((giver == sequence[0]) | (taker == sequence[0]) | (tallies[taker] == 0), 0, jnp.maximum(room, 0))
    moved = jax.random.randint(jax.random.fold_in(own, 4), (count // 2,), 0, 1 << 20) % (room + 1)
    tallies = tallies.at[giver].add(-moved).at[taker].add(moved)
    items = jnp.searchsorted(jnp.cumsum(tallies), jnp.arange(rows * top), side="right").astype(jnp.int32)
    table = items.reshape(top, rows).T
    table = table[jax.random.permutation(jax.random.fold_in(own, 1), rows)]
    offset_by = jax.random.randint(jax.random.fold_in(own, 2), (rows, 1), 0, top)
    return jnp.take_along_axis(table, (jnp.arange(top)[None, :] + offset_by) % top, axis=1)


def shares(number_of, total, most, lean, full):
    portions = [(1 << 20) // math.isqrt(standing ** lean) + 1 for standing in range(1, number_of + 1)]
    largest = most if full else min(most, max(-(-total // number_of), total * portions[0] // sum(portions)))
    least = 1 if total - largest >= number_of - 1 else 0
    given, surplus = [largest] + [least] * (number_of - 1), total - largest - least * (number_of - 1)
    while surplus > 0:
        candidates = [i for i in range(1, number_of) if given[i] < largest] or [i for i in range(1, number_of) if given[i] < most]
        pool, remaining = sum([portions[i] for i in candidates]), surplus
        for i in candidates:
            more = min(most - given[i], max(1, remaining * portions[i] // pool), surplus)
            given[i] = given[i] + more
            surplus = surplus - more
    return np.array(given)


def normal_values(stream_key, dims, spread, bound, pieces=(), kind=jnp.bfloat16):
    level = block_scale(stream_key, dims, pieces, -0.22, 0.18) if pieces else 1.0
    entries = jax.random.normal(stream_key, dims, jnp.float32) * spread * level
    return jnp.minimum(jnp.maximum(entries, -bound), bound).astype(kind)


def setup_inputs(seed: int = 0, part: int = 0) -> dict:
    arg_keys = jax.random.split(jax.random.key(seed), 14)
    own_keys = jax.random.split(jax.random.fold_in(arg_keys[13], part), 14)
    queries = draw_queries(jax.random.fold_in(jax.random.fold_in(arg_keys[13], part), 71), part)
    new_keys = normal_values(own_keys[1], (ROWS, KV_HEADS * HEAD_DIM), 1.0, 6.0, ((0, 16),))
    new_values = normal_values(own_keys[2], (ROWS, KV_HEADS * HEAD_DIM), 1.0, 6.0, ((0, 16),))
    cache_keys = draw_cache_keys(jax.random.fold_in(jax.random.fold_in(arg_keys[13], part), 71), part)
    cache_values = normal_values(own_keys[4], (ROWS, CTX, KV_HEADS * HEAD_DIM), 1.0, 6.0, ((0, 16),))
    lengths = draw_lengths(jax.random.fold_in(jax.random.fold_in(arg_keys[13], part), 71), part)
    norm_gain = jnp.clip(1.0 + 0.1 * jax.random.normal(arg_keys[6], (D,), jnp.float32), 0.5, 1.5)
    route_ids_keys = jax.random.split(jax.random.fold_in(own_keys[7], 1), ROWS // ROWS_DEV)
    route_ids_turns = jax.random.permutation(jax.random.fold_in(own_keys[7], 3), ROWS // ROWS_DEV)
    route_ids = jax.vmap(lambda own, number: shared_out(jax.random.fold_in(own_keys[7], 2), own, number, ROWS_DEV, EXPERTS, 2, CAP, 2))(route_ids_keys, route_ids_turns).reshape((ROWS, 2))
    route_weights = jnp.clip(0.1 + 0.9 * jax.random.uniform(own_keys[8], (ROWS, 2), jnp.float32) ** block_scale(own_keys[8], (ROWS, 2), ((0, 16),), -0.2, 0.2), 0.1, 1.0)
    active_blocks = touch_ends((jax.random.randint(own_keys[9], (EXPERTS, FF // BLOCK), 0, 2) < 1).astype(jnp.int32), jax.random.fold_in(own_keys[9], 1), 0, 1)
    gate_weight = normal_values(arg_keys[10], (EXPERTS * FF, D), D ** -0.5, 0.09375, ((0, 16),))
    up_weight = normal_values(arg_keys[11], (EXPERTS * FF, D), D ** -0.5, 0.09375, ((0, 16),))
    down_weight = normal_values(arg_keys[12], (EXPERTS * FF, D), (FF // 8) ** -0.5, 0.1875, ((0, 16),))
    return dict(queries=queries, new_keys=new_keys, new_values=new_values, cache_keys=cache_keys, cache_values=cache_values, lengths=lengths, norm_gain=norm_gain, route_ids=route_ids, route_weights=route_weights, active_blocks=active_blocks, gate_weight=gate_weight, up_weight=up_weight, down_weight=down_weight)


EPSILON = 1e-05

def rounded(array):
    return lax.optimization_barrier(array.astype(jnp.bfloat16)).astype(jnp.float32)

def attention(queries, new_keys, new_values, cache_keys, cache_values, lengths):
    row_count = queries.shape[0]
    group_size = HEADS // KV_HEADS
    query = queries.astype(jnp.float32).reshape(row_count, KV_HEADS, group_size, HEAD_DIM)
    key_cache = cache_keys.astype(jnp.float32).reshape(row_count, CTX, KV_HEADS, HEAD_DIM)
    value_cache = cache_values.astype(jnp.float32).reshape(row_count, CTX, KV_HEADS, HEAD_DIM)
    own_key = new_keys.astype(jnp.float32).reshape(row_count, KV_HEADS, HEAD_DIM)
    own_value = new_values.astype(jnp.float32).reshape(row_count, KV_HEADS, 1, HEAD_DIM)
    score_scale = HEAD_DIM ** (-0.5)
    cached = jnp.einsum('rkgd,rpkd->rkgp', query, key_cache) * score_scale
    own_score = jnp.einsum('rkgd,rkd->rkg', query, own_key) * score_scale
    valid = lax.broadcasted_iota(jnp.int32, (row_count, CTX), 1) < lengths[:, None]
    cached = jnp.where(valid[:, None, None, :], cached, -jnp.inf)
    row_top = jnp.maximum(lax.optimization_barrier(jnp.max(cached, axis=3)), own_score)
    cached_exp = jnp.exp(cached - row_top[..., None])
    own_exp = jnp.exp(own_score - row_top)
    denominator = lax.optimization_barrier(jnp.sum(cached_exp, axis=3)) + own_exp
    cached_prob = rounded(cached_exp / denominator[..., None])
    own_prob = rounded(own_exp / denominator)
    mixture = jnp.einsum('rkgp,rpkd->rkgd', cached_prob, value_cache) + own_prob[..., None] * own_value
    return mixture.reshape(row_count, HEADS * HEAD_DIM).astype(jnp.bfloat16)

def normalize(attended, norm_gain):
    features = attended.astype(jnp.float32)
    mean_square = lax.optimization_barrier(jnp.mean(features * features, axis=1, keepdims=True))
    return (features * lax.rsqrt(mean_square + EPSILON) * norm_gain[None, :]).astype(jnp.bfloat16)

def pair_ranks(route_ids, experts):
    pair_shape = route_ids.shape
    flat_ids = route_ids.reshape(pair_shape[:-2] + (pair_shape[-2] * 2,))
    onehot = (flat_ids[..., None] == jnp.arange(experts, dtype=jnp.int32)).astype(jnp.int32)
    before = jnp.cumsum(onehot, axis=-2) - onehot
    return lax.optimization_barrier(jnp.sum(before * onehot, axis=-1)).astype(jnp.int32).reshape(pair_shape)

def reference(queries, new_keys, new_values, cache_keys, cache_values, lengths, norm_gain, route_ids, route_weights, active_blocks, gate_weight, up_weight, down_weight):
    attended = attention(queries, new_keys, new_values, cache_keys, cache_values, lengths)
    normed = normalize(attended, norm_gain)
    device_ids = route_ids.reshape(N_EXP, ROWS_DEV, 2)
    pair_rank = pair_ranks(device_ids, EXPERTS)
    expert_iota = jnp.arange(EXPERTS, dtype=jnp.int32)
    slot_iota = jnp.arange(CAP, dtype=jnp.int32)
    slot_match = (device_ids[..., None, None] == expert_iota[:, None]) & (pair_rank[..., None, None] == slot_iota)
    chooser = lax.optimization_barrier(jnp.sum(slot_match.astype(jnp.float32), axis=2))
    row_input = normed.reshape(N_EXP, ROWS_DEV, D).astype(jnp.float32)
    buffers = jnp.einsum('nrec,nrd->encd', chooser, row_input)
    buffers = buffers.reshape(EXPERTS, N_EXP * CAP, D).astype(jnp.bfloat16)
    neuron_mask = jnp.repeat(active_blocks, BLOCK, axis=1).astype(jnp.float32)

    def one_expert(expert_inputs):
        slot_rows, gate_rows, up_rows, down_rows, expert_mask = expert_inputs
        gate_value = lax.dot_general(slot_rows, gate_rows, (((1,), (1,)), ((), ())), preferred_element_type=jnp.float32)
        up_value = lax.dot_general(slot_rows, up_rows, (((1,), (1,)), ((), ())), preferred_element_type=jnp.float32)
        hidden = (jax.nn.relu(gate_value) * jax.nn.relu(up_value) * expert_mask[None, :]).astype(jnp.bfloat16)
        hidden_groups = hidden.reshape(-1, GROUPS, FF_DEV).astype(jnp.float32)
        down_groups = down_rows.reshape(GROUPS, FF_DEV, D).astype(jnp.float32)
        partial_value = rounded(jnp.einsum('sgf,gfd->sgd', hidden_groups, down_groups))
        return lax.optimization_barrier(jnp.sum(partial_value, axis=1))
    results = lax.map(one_expert, (buffers, gate_weight.reshape(EXPERTS, FF, D), up_weight.reshape(EXPERTS, FF, D), down_weight.reshape(EXPERTS, FF, D), neuron_mask))
    results = results.reshape(EXPERTS, N_EXP, CAP, D)
    device_weights = route_weights.reshape(N_EXP, ROWS_DEV, 2)
    row_weights = lax.optimization_barrier(jnp.sum(jnp.where(slot_match, device_weights[..., None, None], 0.0), axis=2))
    expert_out = jnp.einsum('nrec,encd->nrd', row_weights, results, precision=lax.Precision.HIGHEST)
    return (attended, expert_out.reshape(ROWS, D).astype(jnp.bfloat16))
```

```python
import functools

import jax
import jax.numpy as jnp
from jax import lax
from jax.experimental import pallas as pl
from jax.experimental.pallas import tpu as pltpu
from jax.sharding import PartitionSpec as P

KV_HEADS = 8
BLOCK = 128
CAP = 2
EPSILON = 1e-05

QUAD = 4 * BLOCK
SLOTS = 12
EARLY = 6

VMEM = pltpu.VMEM
SMEM = pltpu.SMEM


def slot_of(ids_ref, row, choice):
    mine = ids_ref[row, choice]
    rank = jnp.int32(0)
    for r in range(row + 1):
        for k in range(2):
            if (r, k) < (row, choice):
                rank += (ids_ref[r, k] == mine).astype(jnp.int32)
    return mine * CAP + rank


def attend_kernel(
    lengths_ref, ids_ref, queries_ref, new_keys_ref, new_values_ref, keys_ref, values_ref, gain_ref, attended_ref, outgoing_ref
):
    rows, width = queries_ref.shape
    context = keys_ref.shape[1]
    head_size = new_keys_ref.shape[1] // KV_HEADS
    group = width // head_size // KV_HEADS
    spots = rows * context
    stack = group * rows
    scale = head_size ** (-0.5)
    query = queries_ref[...].astype(jnp.float32)
    new_key = new_keys_ref[...].astype(jnp.float32)
    new_value = new_values_ref[...].astype(jnp.float32)

    scores, owns = [], []
    for j in range(KV_HEADS):
        columns = slice(j * head_size, (j + 1) * head_size)
        heads = [query[:, (j * group + g) * head_size : (j * group + g + 1) * head_size] for g in range(group)]
        stacked = jnp.concatenate(heads, axis=0)
        keys = keys_ref[:, :, columns].reshape(spots, head_size)
        scores.append(
            lax.dot_general(
                stacked.astype(jnp.bfloat16), keys, (((1,), (1,)), ((), ())), preferred_element_type=jnp.float32
            )
        )
        own_key = jnp.concatenate([new_key[:, columns]] * group, axis=0)
        owns.append(jnp.sum(stacked * own_key, axis=1, keepdims=True))
    score = jnp.concatenate(scores, axis=0) * scale
    own = jnp.concatenate(owns, axis=0) * scale
    row_of_line = lax.broadcasted_iota(jnp.int32, score.shape, 0) % rows
    spot = lax.broadcasted_iota(jnp.int32, score.shape, 1)
    valid = jnp.zeros(score.shape, jnp.bool_)
    for r in range(rows):
        valid = valid | ((row_of_line == r) & (spot >= r * context) & (spot < r * context + lengths_ref[r]))
    score = jnp.where(valid, score, -jnp.inf)
    top = jnp.maximum(jnp.max(score, axis=1, keepdims=True), own)
    score_exp = jnp.exp(score - top)
    own_exp = jnp.exp(own - top)
    denominator = jnp.sum(score_exp, axis=1, keepdims=True) + own_exp
    prob = (score_exp / denominator).astype(jnp.bfloat16)
    own_prob = (own_exp / denominator).astype(jnp.bfloat16).astype(jnp.float32)

    pieces = []
    for j in range(KV_HEADS):
        columns = slice(j * head_size, (j + 1) * head_size)
        lines = slice(j * stack, (j + 1) * stack)
        values = values_ref[:, :, columns].reshape(spots, head_size)
        mixture = jnp.dot(prob[lines], values, preferred_element_type=jnp.float32)
        own_value = jnp.concatenate([new_value[:, columns]] * group, axis=0)
        mixture = mixture + own_prob[lines] * own_value
        pieces += [mixture[g * rows : (g + 1) * rows] for g in range(group)]
    attended = jnp.concatenate(pieces, axis=1).astype(jnp.bfloat16)
    attended_ref[...] = attended

    features = attended.astype(jnp.float32)
    mean_square = jnp.mean(features * features, axis=1, keepdims=True)
    normed = features * lax.rsqrt(mean_square + EPSILON) * gain_ref[...]
    normed = normed.astype(jnp.bfloat16).astype(jnp.float32)
    chips = outgoing_ref.shape[0]
    experts = 8
    line = lax.broadcasted_iota(jnp.int32, (experts * CAP, 1), 0)
    packed = jnp.zeros((experts * CAP, width), jnp.float32)
    for r in range(rows):
        chosen = (line == slot_of(ids_ref, r, 0)) | (line == slot_of(ids_ref, r, 1))
        packed = packed + jnp.where(chosen, normed[r : r + 1, :], 0.0)
    packed = packed.astype(jnp.bfloat16)
    for chip in range(chips):
        expert = chip // (chips // experts)
        outgoing_ref[chip] = packed[expert * CAP : (expert + 1) * CAP, :]


def list_blocks(flags_ref, list_ref, blocks):
    experts = flags_ref.shape[0]
    groups = lax.axis_size("exp") // experts
    position = lax.axis_index("exp")
    expert = position // groups
    first = (position % groups) * blocks

    def step(b, count):
        list_ref[count] = b
        return count + (flags_ref[expert, first + b] != 0).astype(jnp.int32)

    return lax.fori_loop(0, blocks, step, jnp.int32(0), unroll=min(blocks, 8))


def item_copies(item, count, list_ref, weights, ring_ref, sems):
    gate_ref, up_ref, down_ref = weights
    pairs = (count + 1) // 2
    slot = item % ring_ref.shape[0]

    def rows(position):
        return pl.ds(pl.multiple_of(list_ref[position] * BLOCK, BLOCK), BLOCK)

    def copy(source_ref, position, part):
        return pltpu.make_async_copy(
            source_ref.at[rows(position), :], ring_ref.at[slot, pl.ds(part * BLOCK, BLOCK), :], sems.at[slot, part]
        )

    def apply(act):
        @pl.when(item < pairs)
        def _():
            for s in range(2):
                @pl.when(2 * item + s < count)
                def _():
                    act(copy(gate_ref, 2 * item + s, s))
                    act(copy(up_ref, 2 * item + s, 2 + s))

        @pl.when(item >= pairs)
        def _():
            for s in range(4):
                position = 4 * (item - pairs) + s
                @pl.when(position < count)
                def _():
                    act(copy(down_ref, position, s))

    return apply


def item_count(count):
    return (count + 1) // 2 + (count + 3) // 4


def preload_kernel(flags_ref, gate_ref, up_ref, down_ref, ring_ref, list_ref, sems):
    blocks = gate_ref.shape[0] // BLOCK
    count = list_blocks(flags_ref, list_ref, blocks)
    weights = (gate_ref, up_ref, down_ref)
    early = jnp.minimum(item_count(count), EARLY)

    def start(item, carry):
        item_copies(item, count, list_ref, weights, ring_ref, sems)(lambda copy: copy.start())
        return carry

    def wait(item, carry):
        item_copies(item, count, list_ref, weights, ring_ref, sems)(lambda copy: copy.wait())
        return carry

    lax.fori_loop(0, early, start, 0)
    lax.fori_loop(0, early, wait, 0)


def experts_kernel(
    flags_ref, near_ref, far_ref, gate_ref, up_ref, down_ref, ring_in, keep_ref, give_ref, ring_ref, list_ref, x_ref, hidden_ref, total_ref, sems
):
    blocks = gate_ref.shape[0] // BLOCK
    half = near_ref.shape[0]
    count = list_blocks(flags_ref, list_ref, blocks)
    weights = (gate_ref, up_ref, down_ref)
    pairs = (count + 1) // 2
    items = item_count(count)

    def act(item, what):
        @pl.when(item < items)
        def _():
            item_copies(item, count, list_ref, weights, ring_ref, sems)(what)

    def start(item, carry):
        act(item, lambda copy: copy.start())
        return carry

    def settle(item):
        @pl.when(item >= EARLY)
        def _():
            act(item, lambda copy: copy.wait())

    lax.fori_loop(EARLY, ring_ref.shape[0], start, 0)
    x_ref[0:half, :] = near_ref[...]
    x_ref[half:, :] = far_ref[...]
    total_ref[...] = jnp.zeros_like(total_ref)

    def project(item, carry):
        settle(item)
        slot = item % ring_ref.shape[0]
        both = lax.dot_general(
            x_ref[...], ring_ref[slot], (((1,), (1,)), ((), ())), preferred_element_type=jnp.float32
        )
        hidden = jax.nn.relu(both[:, : 2 * BLOCK]) * jax.nn.relu(both[:, 2 * BLOCK :])
        neuron = lax.broadcasted_iota(jnp.int32, hidden.shape, 1)
        hidden = jnp.where(neuron < (count - 2 * item) * BLOCK, hidden, 0.0)
        hidden_ref[item] = hidden.astype(jnp.bfloat16)
        start(item + ring_ref.shape[0], 0)
        return carry

    lax.fori_loop(0, pairs, project, 0)

    @pl.when(pairs % 2 == 1)
    def _():
        hidden_ref[pairs] = jnp.zeros(hidden_ref.shape[1:], jnp.bfloat16)

    def contract(chunk, carry):
        item = pairs + chunk
        settle(item)
        slot = item % ring_ref.shape[0]
        for s in range(4):
            @pl.when(4 * chunk + s >= count)
            def _():
                ring_ref[slot, s * BLOCK : (s + 1) * BLOCK, :] = jnp.zeros((BLOCK, ring_ref.shape[2]), jnp.bfloat16)

        hidden = jnp.concatenate([hidden_ref[2 * chunk], hidden_ref[2 * chunk + 1]], axis=1)
        total_ref[...] += jnp.dot(hidden, ring_ref[slot], preferred_element_type=jnp.float32)
        start(item + ring_ref.shape[0], 0)
        return carry

    lax.fori_loop(0, items - pairs, contract, 0)
    keep_ref[...] = total_ref[0:half, :]
    give_ref[...] = total_ref[half:, :].astype(jnp.bfloat16)


def combine_kernel(ids_ref, route_weights_ref, returned_ref, out_ref):
    rows = out_ref.shape[0]
    chips = returned_ref.shape[0]
    experts = 8
    share = chips // experts
    line = lax.broadcasted_iota(jnp.int32, (rows, 1), 0)
    slots = [[slot_of(ids_ref, r, k) for k in range(2)] for r in range(rows)]
    total = jnp.zeros(out_ref.shape, jnp.float32)
    for expert in range(experts):
        value = returned_ref[expert * share].astype(jnp.float32)
        for part in range(1, share):
            value = value + returned_ref[expert * share + part].astype(jnp.float32)
        for c in range(CAP):
            weight = jnp.zeros((rows, 1), jnp.float32)
            for r in range(rows):
                for k in range(2):
                    hit = (slots[r][k] == expert * CAP + c).astype(jnp.float32)
                    weight = jnp.where(line == r, weight + hit * route_weights_ref[r, k], weight)
            total = total + weight * value[c : c + 1, :]
    out_ref[...] = total.astype(jnp.bfloat16)


def shards(
    queries,
    new_keys,
    new_values,
    cache_keys,
    cache_values,
    lengths,
    norm_gain,
    route_ids,
    route_weights,
    active_blocks,
    gate_weight,
    up_weight,
    down_weight,
):
    devices = lax.axis_size("exp")
    chips = devices // 2
    width = queries.shape[1]
    half = chips * CAP
    blocks = gate_weight.shape[0] // BLOCK
    same_core = [[2 * chip + core for chip in range(chips)] for core in range(2)]
    core_swap = [(device, device ^ 1) for device in range(devices)]
    vmem = pl.BlockSpec(memory_space=VMEM)
    smem = pl.BlockSpec(memory_space=SMEM)
    hbm = pl.BlockSpec(memory_space=pl.ANY)
    slots = min(SLOTS, (blocks + 1) // 2 + (blocks + 3) // 4)
    ring_shape = (slots, QUAD, width)

    attended, outgoing = pl.pallas_call(
        attend_kernel,
        out_shape=(
            jax.ShapeDtypeStruct(queries.shape, jnp.bfloat16),
            jax.ShapeDtypeStruct((chips, CAP, width), jnp.bfloat16),
        ),
        in_specs=[smem, smem] + [vmem] * 6,
        out_specs=(vmem, vmem),
        name="attend",
    )(lengths, route_ids, queries, new_keys, new_values, cache_keys, cache_values, norm_gain[None, :])

    def exchange(array):
        return lax.all_to_all(array, "exp", split_axis=0, concat_axis=0, tiled=True, axis_index_groups=same_core)

    ring = pl.pallas_call(
        preload_kernel,
        out_shape=pltpu.VMEM(ring_shape, jnp.bfloat16),
        in_specs=[smem, hbm, hbm, hbm],
        out_specs=vmem,
        scratch_shapes=[pltpu.SMEM((blocks,), jnp.int32), pltpu.SemaphoreType.DMA((slots, 4))],
        compiler_params=pltpu.CompilerParams(vmem_limit_bytes=2 * 2**20),
        cost_estimate=pl.CostEstimate(flops=0, transcendentals=0, bytes_accessed=EARLY * QUAD * width * 2),
        name="preload",
    )(active_blocks, gate_weight, up_weight, down_weight)

    near = exchange(outgoing).reshape(half, width)
    far = lax.ppermute(near, "exp", core_swap)

    keep, give, _ = pl.pallas_call(
        experts_kernel,
        out_shape=(
            jax.ShapeDtypeStruct((half, width), jnp.float32),
            jax.ShapeDtypeStruct((half, width), jnp.bfloat16),
            pltpu.VMEM(ring_shape, jnp.bfloat16),
        ),
        in_specs=[smem, vmem, vmem, hbm, hbm, hbm, vmem],
        out_specs=(vmem, vmem, vmem),
        scratch_shapes=[
            pltpu.SMEM((blocks,), jnp.int32),
            pltpu.VMEM((2 * half, width), jnp.bfloat16),
            pltpu.VMEM((blocks // 2 + 1, 2 * half, 2 * BLOCK), jnp.bfloat16),
            pltpu.VMEM((2 * half, width), jnp.float32),
            pltpu.SemaphoreType.DMA((slots, 4)),
        ],
        input_output_aliases={6: 2},
        compiler_params=pltpu.CompilerParams(vmem_limit_bytes=6 * 2**20 + 16 * half * width),
        name="experts",
    )(active_blocks, near, far, gate_weight, up_weight, down_weight, ring)

    from_core = lax.ppermute(give, "exp", core_swap)
    partial_value = (keep + from_core.astype(jnp.float32)).astype(jnp.bfloat16)
    returned = exchange(partial_value.reshape(chips, CAP, width))
    expert_out = pl.pallas_call(
        combine_kernel,
        out_shape=jax.ShapeDtypeStruct(queries.shape, jnp.bfloat16),
        in_specs=[smem, smem, vmem],
        out_specs=vmem,
        name="combine",
    )(route_ids, route_weights, returned)
    return attended, expert_out


def solution(mesh):
    rows = P(("dom", "exp"), None)
    return jax.shard_map(
        shards,
        mesh=mesh,
        in_specs=(
            rows,
            rows,
            rows,
            P(("dom", "exp"), None, None),
            P(("dom", "exp"), None, None),
            P(("dom", "exp")),
            P(),
            rows,
            rows,
            P("dom", None),
            P("exp", None),
            P("exp", None),
            P("exp", None),
        ),
        out_specs=(rows, rows),
        check_vma=False,
    )
```

```python
import math

import jax
import jax.numpy as jnp
from jax import lax
from jax.experimental import pallas as pl
from jax.experimental.pallas import tpu as pltpu
from jax.sharding import PartitionSpec as P

KV_HEADS = 8
BLOCK = 128
CAP = 2
EPSILON = 1e-05

QUAD = 4 * BLOCK
SLOTS = 8

WIDE = 1
ORIENT = 2

vmem = pl.BlockSpec(memory_space=pltpu.VMEM)
smem = pl.BlockSpec(memory_space=pltpu.SMEM)
hbm = pl.BlockSpec(memory_space=pl.ANY)


def slot_of(ids_ref, row, choice):
    mine = ids_ref[choice, row]
    rank = jnp.int32(0)
    for r in range(row + 1):
        for k in range(2):
            if (r, k) < (row, choice):
                rank += (ids_ref[k, r] == mine).astype(jnp.int32)
    return mine * CAP + rank


def attend_kernel(
    lengths_ref,
    ids_ref,
    route_weights_ref,
    flags_ref,
    queries_ref,
    new_keys_ref,
    new_values_ref,
    keys_ref,
    values_ref,
    gain_ref,
    attended_ref,
    outgoing_ref,
    mix_ref,
    list_ref,
):
    rows, width = queries_ref.shape
    context = keys_ref.shape[1]
    head_size = new_keys_ref.shape[1] // KV_HEADS
    group = width // head_size // KV_HEADS
    spots = rows * context
    stack = group * rows
    scale = head_size ** (-0.5)
    list_blocks(flags_ref, list_ref, list_ref.shape[1] - 1)
    query = queries_ref[...].astype(jnp.float32)
    new_key = new_keys_ref[...].astype(jnp.float32)
    new_value = new_values_ref[...].astype(jnp.float32)

    scores, owns = [], []
    for j in range(KV_HEADS):
        columns = slice(j * head_size, (j + 1) * head_size)
        heads = [query[:, (j * group + g) * head_size : (j * group + g + 1) * head_size] for g in range(group)]
        stacked = jnp.concatenate(heads, axis=0)
        keys = keys_ref[:, :, columns].reshape(spots, head_size)
        scores.append(
            lax.dot_general(
                stacked.astype(jnp.bfloat16), keys, (((1,), (1,)), ((), ())), preferred_element_type=jnp.float32
            )
        )
        own_key = jnp.concatenate([new_key[:, columns]] * group, axis=0)
        owns.append(jnp.sum(stacked * own_key, axis=1, keepdims=True))
    score = jnp.concatenate(scores, axis=0) * scale
    own = jnp.concatenate(owns, axis=0) * scale
    row_of_line = lax.broadcasted_iota(jnp.int32, score.shape, 0) % rows
    spot = lax.broadcasted_iota(jnp.int32, score.shape, 1)
    valid = jnp.zeros(score.shape, jnp.bool_)
    for r in range(rows):
        valid = valid | ((row_of_line == r) & (spot >= r * context) & (spot < r * context + lengths_ref[r]))
    score = jnp.where(valid, score, -jnp.inf)
    top = jnp.maximum(jnp.max(score, axis=1, keepdims=True), own)
    score_exp = jnp.exp(score - top)
    own_exp = jnp.exp(own - top)
    denominator = jnp.sum(score_exp, axis=1, keepdims=True) + own_exp
    prob = (score_exp / denominator).astype(jnp.bfloat16)
    own_prob = (own_exp / denominator).astype(jnp.bfloat16).astype(jnp.float32)

    pieces = []
    for j in range(KV_HEADS):
        columns = slice(j * head_size, (j + 1) * head_size)
        lines = slice(j * stack, (j + 1) * stack)
        values = values_ref[:, :, columns].reshape(spots, head_size)
        mixture = jnp.dot(prob[lines], values, preferred_element_type=jnp.float32)
        own_value = jnp.concatenate([new_value[:, columns]] * group, axis=0)
        mixture = mixture + own_prob[lines] * own_value
        pieces += [mixture[g * rows : (g + 1) * rows] for g in range(group)]
    attended = jnp.concatenate(pieces, axis=1).astype(jnp.bfloat16)
    attended_ref[...] = attended

    features = attended.astype(jnp.float32)
    mean_square = jnp.mean(features * features, axis=1, keepdims=True)
    normed = features * lax.rsqrt(mean_square + EPSILON) * gain_ref[...]
    normed = normed.astype(jnp.bfloat16).astype(jnp.float32)
    chips = outgoing_ref.shape[0]
    experts = flags_ref.shape[0]
    line = lax.broadcasted_iota(jnp.int32, (experts * CAP, 1), 0)
    mix_row = lax.broadcasted_iota(jnp.int32, mix_ref.shape, 0)
    mix_slot = lax.broadcasted_iota(jnp.int32, mix_ref.shape, 1)
    packed = jnp.zeros((experts * CAP, width), jnp.float32)
    mix = jnp.zeros(mix_ref.shape, jnp.float32)
    for r in range(rows):
        slots = [slot_of(ids_ref, r, k) for k in range(2)]
        packed = packed + jnp.where((line == slots[0]) | (line == slots[1]), normed[r : r + 1, :], 0.0)
        for k in range(2):
            mix = mix + jnp.where((mix_row == r) & (mix_slot == slots[k]), route_weights_ref[k, r], 0.0)
    packed = packed.astype(jnp.bfloat16)
    for chip in range(chips):
        expert = chip // (chips // experts)
        outgoing_ref[chip] = packed[expert * CAP : (expert + 1) * CAP, :]
    mix_ref[...] = mix


def list_blocks(flags_ref, list_ref, blocks):
    experts = flags_ref.shape[0]
    groups = lax.axis_size("exp") // experts
    position = lax.axis_index("exp")
    expert = position // groups
    first = (position % groups) * blocks

    count = jnp.int32(0)
    for b in range(blocks):
        list_ref[0, count] = b
        count += (flags_ref[expert, first + b] != 0).astype(jnp.int32)
    list_ref[0, blocks] = count


def item_copies(item, count, list_ref, weights, ring_ref, sems):
    gate_ref, up_ref, down_ref = weights
    pairs = (count + 1) // 2
    first_down = pairs
    slot = item % ring_ref.shape[0]

    def copy(source_ref, position, part):
        rows = pl.ds(pl.multiple_of(list_ref[0, position] * BLOCK, BLOCK), BLOCK)
        return pltpu.make_async_copy(
            source_ref.at[rows, :], ring_ref.at[slot, pl.ds(part * BLOCK, BLOCK), :], sems.at[slot, part]
        )

    def apply(act):
        @pl.when(item < pairs)
        def _():
            for s in range(2):
                @pl.when(2 * item + s < count)
                def _():
                    act(copy(gate_ref, 2 * item + s, s))
                    act(copy(up_ref, 2 * item + s, 2 + s))

        @pl.when(item >= first_down)
        def _():
            for s in range(2):
                position = 2 * (item - first_down) + s
                @pl.when(position < count)
                def _():
                    act(copy(down_ref, position, s))

    return apply


def experts_kernel(
    list_ref,
    near_ref,
    far_ref,
    attended_ref,
    gate_ref,
    up_ref,
    down_ref,
    keep_ref,
    give_ref,
    attended_out,
    ring_ref,
    x_ref,
    hidden_ref,
    total_ref,
    sems,
    attended_sem,
):
    blocks = gate_ref.shape[0] // BLOCK
    half = near_ref.shape[0]
    ring_slots = ring_ref.shape[0]
    count = list_ref[0, blocks]
    weights = (gate_ref, up_ref, down_ref)
    pairs = (count + 1) // 2
    chunks = (count + 1) // 2
    first_down = pairs

    def start(item, carry):
        item_copies(item, count, list_ref, weights, ring_ref, sems)(lambda copy: copy.start())
        return carry

    def settle(item):
        item_copies(item, count, list_ref, weights, ring_ref, sems)(lambda copy: copy.wait())

    lax.fori_loop(0, ring_slots, start, 0)
    write = pltpu.make_async_copy(attended_ref, attended_out, attended_sem)
    write.start()
    x_ref[0:half, :] = near_ref[...]
    x_ref[half:, :] = far_ref[...]
    total_ref[...] = jnp.zeros_like(total_ref)

    def project(first, number):
        for i in range(number):
            settle(first + i)
        for i in range(number):
            item = first + i
            slot = item % ring_slots
            if ORIENT == 1:
                both = lax.dot_general(
                    x_ref[...], ring_ref[slot], (((1,), (1,)), ((), ())), preferred_element_type=jnp.float32
                )
                hidden = jax.nn.relu(both[:, : 2 * BLOCK]) * jax.nn.relu(both[:, 2 * BLOCK :])
            else:
                both = lax.dot_general(
                    ring_ref[slot], x_ref[...], (((1,), (1,)), ((), ())), preferred_element_type=jnp.float32
                )
                hidden = (jax.nn.relu(both[: 2 * BLOCK]) * jax.nn.relu(both[2 * BLOCK :])).T
            neuron = lax.broadcasted_iota(jnp.int32, hidden.shape, 1)
            hidden = jnp.where(neuron < (count - 2 * item) * BLOCK, hidden, 0.0)
            hidden_ref[item] = hidden.astype(jnp.bfloat16)
        for i in range(number):
            start(first + i + ring_slots, 0)

    def contract(first, number):
        for i in range(number):
            settle(first_down + first + i)

            @pl.when(2 * (first + i) + 1 == count)
            def _():
                ring_ref[(first_down + first + i) % ring_slots, BLOCK : 2 * BLOCK, :] = jnp.zeros(
                    (BLOCK, ring_ref.shape[2]), jnp.bfloat16
                )

        for i in range(number):
            rows = ring_ref[(first_down + first + i) % ring_slots, : 2 * BLOCK, :]
            total_ref[...] += jnp.dot(hidden_ref[first + i], rows, preferred_element_type=jnp.float32)
        for i in range(number):
            start(first_down + first + i + ring_slots, 0)

    def steps(body, number):
        whole = number // WIDE

        def wide(step, carry):
            body(WIDE * step, WIDE)
            return carry

        def single(step, carry):
            body(step, 1)
            return carry

        lax.fori_loop(0, whole, wide, 0)
        lax.fori_loop(WIDE * whole, number, single, 0)

    steps(project, pairs)

    steps(contract, chunks)
    keep_ref[...] = total_ref[0:half, :]
    give_ref[...] = total_ref[half:, :].astype(jnp.bfloat16)
    write.wait()


def merge_kernel(keep_ref, taken_ref, out_ref):
    total = (keep_ref[...] + taken_ref[...].astype(jnp.float32)).astype(jnp.bfloat16)
    for chip in range(out_ref.shape[0]):
        out_ref[chip] = total[chip * CAP : (chip + 1) * CAP, :]


def combine_kernel(mix_ref, returned_ref, out_ref):
    rows = out_ref.shape[0]
    experts = mix_ref.shape[1] // CAP
    share = returned_ref.shape[0] // experts
    mix = mix_ref[...]
    total = jnp.zeros(out_ref.shape, jnp.float32)
    for expert in range(experts):
        value = returned_ref[expert * share].astype(jnp.float32)
        for part in range(1, share):
            value = value + returned_ref[expert * share + part].astype(jnp.float32)
        for c in range(CAP):
            slot = expert * CAP + c
            total = total + mix[0:rows, slot : slot + 1] * value[c : c + 1, :]
    out_ref[...] = total.astype(jnp.bfloat16)


def ring_of(gate_weight):
    blocks, width = gate_weight.shape[0] // BLOCK, gate_weight.shape[1]
    slots = min(SLOTS, (blocks + 1) // 2 * 2)
    return blocks, (slots, QUAD, width)


def in_vmem(array):
    return pltpu.with_memory_space_constraint(array, pltpu.VMEM)


def experts(listing, near, far, attended, gate_weight, up_weight, down_weight):
    blocks, ring_shape = ring_of(gate_weight)
    half, width = near.shape
    return pl.pallas_call(
        experts_kernel,
        out_shape=(
            pltpu.VMEM((half, width), jnp.float32),
            pltpu.VMEM((half, width), jnp.bfloat16),
            jax.ShapeDtypeStruct(attended.shape, jnp.bfloat16),
        ),
        in_specs=[smem, vmem, vmem, vmem, hbm, hbm, hbm],
        out_specs=(vmem, vmem, hbm),
        scratch_shapes=[
            pltpu.VMEM(ring_shape, jnp.bfloat16),
            pltpu.VMEM((2 * half, width), jnp.bfloat16),
            pltpu.VMEM(((blocks + 1) // 2, 2 * half, 2 * BLOCK), jnp.bfloat16),
            pltpu.VMEM((2 * half, width), jnp.float32),
            pltpu.SemaphoreType.DMA((ring_shape[0], 4)),
            pltpu.SemaphoreType.DMA,
        ],
        compiler_params=pltpu.CompilerParams(vmem_limit_bytes=6 * 2**20 + 16 * half * width + 2 * math.prod(ring_shape)),
        name="experts",
    )(pltpu.with_memory_space_constraint(listing, pltpu.SMEM), in_vmem(near), in_vmem(far), in_vmem(attended), gate_weight, up_weight, down_weight)


def shards(
    queries,
    new_keys,
    new_values,
    cache_keys,
    cache_values,
    lengths,
    norm_gain,
    route_ids,
    route_weights,
    active_blocks,
    gate_weight,
    up_weight,
    down_weight,
):
    devices = lax.axis_size("exp")
    chips = devices // 2
    width = queries.shape[1]
    half = chips * CAP
    same_core = [[2 * chip + core for chip in range(chips)] for core in range(2)]
    core_swap = [(device, device ^ 1) for device in range(devices)]

    experts_number = active_blocks.shape[0]
    attended, outgoing, mix, listing = pl.pallas_call(
        attend_kernel,
        out_shape=(
            pltpu.VMEM(queries.shape, jnp.bfloat16),
            pltpu.VMEM((chips, CAP, width), jnp.bfloat16),
            pltpu.VMEM((8, experts_number * CAP), jnp.float32),
            pltpu.SMEM((1, gate_weight.shape[0] // BLOCK + 1), jnp.int32),
        ),
        in_specs=[smem] * 4 + [vmem] * 6,
        out_specs=(vmem, vmem, vmem, smem),
        name="attend",
    )(
        lengths,
        route_ids.T,
        route_weights.T,
        active_blocks,
        queries,
        new_keys,
        new_values,
        cache_keys,
        cache_values,
        norm_gain[None, :],
    )

    def exchange(array):
        return lax.all_to_all(array, "exp", split_axis=0, concat_axis=0, tiled=True, axis_index_groups=same_core)

    near = exchange(outgoing).reshape(half, width)
    far = lax.ppermute(near, "exp", core_swap)

    keep, give, attended = experts(listing, near, far, attended, gate_weight, up_weight, down_weight)
    taken = lax.ppermute(give, "exp", core_swap)
    merged = pl.pallas_call(
        merge_kernel,
        out_shape=pltpu.VMEM((chips, CAP, width), jnp.bfloat16),
        in_specs=[vmem, vmem],
        out_specs=vmem,
        name="merge",
    )(in_vmem(keep), in_vmem(taken))
    returned = exchange(merged)
    expert_out = pl.pallas_call(
        combine_kernel,
        out_shape=jax.ShapeDtypeStruct(queries.shape, jnp.bfloat16),
        in_specs=[vmem, vmem],
        out_specs=vmem,
        name="combine",
    )(in_vmem(mix), in_vmem(returned))
    return attended, expert_out


def solution(mesh):
    rows = P(("dom", "exp"), None)
    return jax.shard_map(
        shards,
        mesh=mesh,
        in_specs=(
            rows,
            rows,
            rows,
            P(("dom", "exp"), None, None),
            P(("dom", "exp"), None, None),
            P(("dom", "exp")),
            P(),
            rows,
            rows,
            P("dom", None),
            P("exp", None),
            P("exp", None),
            P("exp", None),
        ),
        out_specs=(rows, rows),
        check_vma=False,
    )
```

```python
import math

import jax
import jax.numpy as jnp
from jax import lax
from jax.experimental import pallas as pl
from jax.experimental.pallas import tpu as pltpu
from jax.sharding import PartitionSpec as P

KV_HEADS = 8
BLOCK = 128
CAP = 2
EPSILON = 1e-05

QUAD = 4 * BLOCK
SLOTS = 8

FWD16 = False
RET16 = False

vmem = pl.BlockSpec(memory_space=pltpu.VMEM)
smem = pl.BlockSpec(memory_space=pltpu.SMEM)
hbm = pl.BlockSpec(memory_space=pl.ANY)


def slot_of(ids_ref, row, choice):
    mine = ids_ref[choice, row]
    rank = jnp.int32(0)
    for r in range(row + 1):
        for k in range(2):
            if (r, k) < (row, choice):
                rank += (ids_ref[k, r] == mine).astype(jnp.int32)
    return mine * CAP + rank


def attend_kernel(
    lengths_ref,
    ids_ref,
    route_weights_ref,
    flags_ref,
    queries_ref,
    new_keys_ref,
    new_values_ref,
    keys_ref,
    values_ref,
    gain_ref,
    attended_ref,
    outgoing_ref,
    mix_ref,
    list_ref,
):
    rows, width = queries_ref.shape
    context = keys_ref.shape[1]
    head_size = new_keys_ref.shape[1] // KV_HEADS
    group = width // head_size // KV_HEADS
    spots = rows * context
    stack = group * rows
    scale = head_size ** (-0.5)
    list_blocks(flags_ref, list_ref, list_ref.shape[1] - 1)
    query = queries_ref[...].astype(jnp.float32)
    new_key = new_keys_ref[...].astype(jnp.float32)
    new_value = new_values_ref[...].astype(jnp.float32)

    scores, owns = [], []
    for j in range(KV_HEADS):
        columns = slice(j * head_size, (j + 1) * head_size)
        heads = [query[:, (j * group + g) * head_size : (j * group + g + 1) * head_size] for g in range(group)]
        stacked = jnp.concatenate(heads, axis=0)
        keys = keys_ref[:, :, columns].reshape(spots, head_size)
        scores.append(
            lax.dot_general(
                stacked.astype(jnp.bfloat16), keys, (((1,), (1,)), ((), ())), preferred_element_type=jnp.float32
            )
        )
        own_key = jnp.concatenate([new_key[:, columns]] * group, axis=0)
        owns.append(jnp.sum(stacked * own_key, axis=1, keepdims=True))
    score = jnp.concatenate(scores, axis=0) * scale
    own = jnp.concatenate(owns, axis=0) * scale
    row_of_line = lax.broadcasted_iota(jnp.int32, score.shape, 0) % rows
    spot = lax.broadcasted_iota(jnp.int32, score.shape, 1)
    valid = jnp.zeros(score.shape, jnp.bool_)
    for r in range(rows):
        valid = valid | ((row_of_line == r) & (spot >= r * context) & (spot < r * context + lengths_ref[r]))
    score = jnp.where(valid, score, -jnp.inf)
    top = jnp.maximum(jnp.max(score, axis=1, keepdims=True), own)
    score_exp = jnp.exp(score - top)
    own_exp = jnp.exp(own - top)
    denominator = jnp.sum(score_exp, axis=1, keepdims=True) + own_exp
    prob = (score_exp / denominator).astype(jnp.bfloat16)
    own_prob = (own_exp / denominator).astype(jnp.bfloat16).astype(jnp.float32)

    pieces = []
    for j in range(KV_HEADS):
        columns = slice(j * head_size, (j + 1) * head_size)
        lines = slice(j * stack, (j + 1) * stack)
        values = values_ref[:, :, columns].reshape(spots, head_size)
        mixture = jnp.dot(prob[lines], values, preferred_element_type=jnp.float32)
        own_value = jnp.concatenate([new_value[:, columns]] * group, axis=0)
        mixture = mixture + own_prob[lines] * own_value
        pieces += [mixture[g * rows : (g + 1) * rows] for g in range(group)]
    attended = jnp.concatenate(pieces, axis=1).astype(jnp.bfloat16)
    attended_ref[...] = attended

    features = attended.astype(jnp.float32)
    mean_square = jnp.mean(features * features, axis=1, keepdims=True)
    normed = features * lax.rsqrt(mean_square + EPSILON) * gain_ref[...]
    normed = normed.astype(jnp.bfloat16).astype(jnp.float32)
    places = outgoing_ref.shape[0]
    experts = flags_ref.shape[0]
    line = lax.broadcasted_iota(jnp.int32, (experts * CAP, 1), 0)
    mix_row = lax.broadcasted_iota(jnp.int32, mix_ref.shape, 0)
    mix_slot = lax.broadcasted_iota(jnp.int32, mix_ref.shape, 1)
    packed = jnp.zeros((experts * CAP, width), jnp.float32)
    mix = jnp.zeros(mix_ref.shape, jnp.float32)
    for r in range(rows):
        slots = [slot_of(ids_ref, r, k) for k in range(2)]
        packed = packed + jnp.where((line == slots[0]) | (line == slots[1]), normed[r : r + 1, :], 0.0)
        for k in range(2):
            mix = mix + jnp.where((mix_row == r) & (mix_slot == slots[k]), route_weights_ref[k, r], 0.0)
    packed = packed.astype(jnp.bfloat16)
    for place in range(places):
        expert = place // (places // experts)
        outgoing_ref[place] = packed[expert * CAP : (expert + 1) * CAP, :]
    mix_ref[...] = mix


def list_blocks(flags_ref, list_ref, blocks):
    experts = flags_ref.shape[0]
    groups = lax.axis_size("exp") // experts
    position = lax.axis_index("exp")
    expert = position // groups
    first = (position % groups) * blocks

    count = jnp.int32(0)
    for b in range(blocks):
        list_ref[0, count] = b
        count += (flags_ref[expert, first + b] != 0).astype(jnp.int32)
    list_ref[0, blocks] = count


def item_copies(item, count, list_ref, weights, ring_ref, sems):
    gate_ref, up_ref, down_ref = weights
    pairs = (count + 1) // 2
    slot = item % ring_ref.shape[0]

    def copy(source_ref, position, part):
        rows = pl.ds(pl.multiple_of(list_ref[0, position] * BLOCK, BLOCK), BLOCK)
        return pltpu.make_async_copy(
            source_ref.at[rows, :], ring_ref.at[slot, pl.ds(part * BLOCK, BLOCK), :], sems.at[slot, part]
        )

    def apply(act):
        @pl.when(item < pairs)
        def _():
            for s in range(2):
                @pl.when(2 * item + s < count)
                def _():
                    act(copy(gate_ref, 2 * item + s, 2 * s))
                    act(copy(up_ref, 2 * item + s, 2 * s + 1))

        @pl.when(item >= pairs)
        def _():
            for s in range(2):
                position = 2 * (item - pairs) + s
                @pl.when(position < count)
                def _():
                    act(copy(down_ref, position, s))

    return apply


def experts_kernel(
    list_ref,
    near_ref,
    far_ref,
    attended_ref,
    gate_ref,
    up_ref,
    down_ref,
    keep_ref,
    give_ref,
    attended_out,
    ring_ref,
    x_ref,
    hidden_ref,
    total_ref,
    sems,
    attended_sem,
):
    blocks = gate_ref.shape[0] // BLOCK
    core = lax.axis_index("exp") % 2
    chips = x_ref.shape[0] // (2 * CAP)
    half = chips * CAP
    ring_slots = ring_ref.shape[0]
    count = list_ref[0, blocks]
    weights = (gate_ref, up_ref, down_ref)
    whole = count // 2
    pairs = (count + 1) // 2

    def start(item, carry):
        item_copies(item, count, list_ref, weights, ring_ref, sems)(lambda copy: copy.start())
        return carry

    def settle(item):
        item_copies(item, count, list_ref, weights, ring_ref, sems)(lambda copy: copy.wait())

    lax.fori_loop(0, ring_slots, start, 0)
    write = pltpu.make_async_copy(attended_ref, attended_out, attended_sem)
    write.start()
    for chip in range(chips):
        x_ref[chip * CAP : (chip + 1) * CAP, :] = near_ref[2 * chip + core] if FWD16 else near_ref[chip]
        x_ref[half + chip * CAP : half + (chip + 1) * CAP, :] = near_ref[2 * chip + 1 - core] if FWD16 else far_ref[chip]
    total_ref[...] = jnp.zeros_like(total_ref)

    def project(item, number):
        settle(item)
        slot = item % ring_slots
        both = lax.dot_general(
            ring_ref[slot, : 2 * number * BLOCK, :],
            x_ref[...],
            (((1,), (1,)), ((), ())),
            preferred_element_type=jnp.float32,
        )
        for s in range(number):
            gate = both[2 * s * BLOCK : (2 * s + 1) * BLOCK]
            up = both[(2 * s + 1) * BLOCK : (2 * s + 2) * BLOCK]
            hidden = (jax.nn.relu(gate) * jax.nn.relu(up)).T
            hidden_ref[item, :, s * BLOCK : (s + 1) * BLOCK] = hidden.astype(jnp.bfloat16)
        start(item + ring_slots, 0)

    def contract(chunk, number):
        item = pairs + chunk
        settle(item)
        total_ref[...] += jnp.dot(
            hidden_ref[chunk, :, : number * BLOCK],
            ring_ref[item % ring_slots, : number * BLOCK, :],
            preferred_element_type=jnp.float32,
        )
        start(item + ring_slots, 0)

    def steps(body):
        def pair(step, carry):
            body(step, 2)
            return carry

        lax.fori_loop(0, whole, pair, 0)

        @pl.when(whole < pairs)
        def _():
            body(whole, 1)

    steps(project)
    steps(contract)
    if RET16:
        for chip in range(chips):
            give_ref[2 * chip + core] = total_ref[chip * CAP : (chip + 1) * CAP, :].astype(jnp.bfloat16)
            give_ref[2 * chip + 1 - core] = total_ref[half + chip * CAP : half + (chip + 1) * CAP, :].astype(jnp.bfloat16)
    else:
        keep_ref[...] = total_ref[0:half, :]
        give_ref[...] = total_ref[half:, :].astype(jnp.bfloat16)
    write.wait()


def merge_kernel(keep_ref, taken_ref, out_ref):
    total = (keep_ref[...] + taken_ref[...].astype(jnp.float32)).astype(jnp.bfloat16)
    for chip in range(out_ref.shape[0]):
        out_ref[chip] = total[chip * CAP : (chip + 1) * CAP, :]


def combine_kernel(mix_ref, returned_ref, out_ref):
    rows = out_ref.shape[0]
    experts = mix_ref.shape[1] // CAP
    share = returned_ref.shape[0] // experts
    mix = mix_ref[...]
    total = jnp.zeros(out_ref.shape, jnp.float32)
    for expert in range(experts):
        value = returned_ref[expert * share].astype(jnp.float32)
        for part in range(1, share):
            value = value + returned_ref[expert * share + part].astype(jnp.float32)
        for c in range(CAP):
            slot = expert * CAP + c
            total = total + mix[0:rows, slot : slot + 1] * value[c : c + 1, :]
    out_ref[...] = total.astype(jnp.bfloat16)


def ring_of(gate_weight):
    blocks, width = gate_weight.shape[0] // BLOCK, gate_weight.shape[1]
    slots = min(SLOTS, (blocks + 1) // 2 * 2)
    return blocks, (slots, QUAD, width)


def in_vmem(array):
    return pltpu.with_memory_space_constraint(array, pltpu.VMEM)


def experts(listing, near, far, attended, gate_weight, up_weight, down_weight):
    blocks, ring_shape = ring_of(gate_weight)
    half, width = lax.axis_size("exp") // 2 * CAP, near.shape[2]
    return pl.pallas_call(
        experts_kernel,
        out_shape=(
            pltpu.VMEM((8, 128) if RET16 else (half, width), jnp.float32),
            pltpu.VMEM((half, CAP, width) if RET16 else (half, width), jnp.bfloat16),
            jax.ShapeDtypeStruct(attended.shape, jnp.bfloat16),
        ),
        in_specs=[smem, vmem, vmem, vmem, hbm, hbm, hbm],
        out_specs=(vmem, vmem, hbm),
        scratch_shapes=[
            pltpu.VMEM(ring_shape, jnp.bfloat16),
            pltpu.VMEM((2 * half, width), jnp.bfloat16),
            pltpu.VMEM(((blocks + 1) // 2, 2 * half, 2 * BLOCK), jnp.bfloat16),
            pltpu.VMEM((2 * half, width), jnp.float32),
            pltpu.SemaphoreType.DMA((ring_shape[0], 4)),
            pltpu.SemaphoreType.DMA,
        ],
        compiler_params=pltpu.CompilerParams(vmem_limit_bytes=6 * 2**20 + 16 * half * width + 2 * math.prod(ring_shape)),
        name="experts",
    )(pltpu.with_memory_space_constraint(listing, pltpu.SMEM), in_vmem(near), in_vmem(far), in_vmem(attended), gate_weight, up_weight, down_weight)


def shards(
    queries,
    new_keys,
    new_values,
    cache_keys,
    cache_values,
    lengths,
    norm_gain,
    route_ids,
    route_weights,
    active_blocks,
    gate_weight,
    up_weight,
    down_weight,
):
    devices = lax.axis_size("exp")
    chips = devices // 2
    width = queries.shape[1]
    half = chips * CAP
    same_core = [[2 * chip + core for chip in range(chips)] for core in range(2)]
    core_swap = [(device, device ^ 1) for device in range(devices)]

    experts_number = active_blocks.shape[0]
    attended, outgoing, mix, listing = pl.pallas_call(
        attend_kernel,
        out_shape=(
            pltpu.VMEM(queries.shape, jnp.bfloat16),
            pltpu.VMEM((devices if FWD16 else chips, CAP, width), jnp.bfloat16),
            pltpu.VMEM((8, experts_number * CAP), jnp.float32),
            pltpu.SMEM((1, gate_weight.shape[0] // BLOCK + 1), jnp.int32),
        ),
        in_specs=[smem] * 4 + [vmem] * 6,
        out_specs=(vmem, vmem, vmem, smem),
        name="attend",
    )(
        lengths,
        route_ids.T,
        route_weights.T,
        active_blocks,
        queries,
        new_keys,
        new_values,
        cache_keys,
        cache_values,
        norm_gain[None, :],
    )

    def exchange(array):
        return lax.all_to_all(array, "exp", split_axis=0, concat_axis=0, tiled=True, axis_index_groups=same_core)

    if FWD16:
        near = lax.all_to_all(outgoing, "exp", split_axis=0, concat_axis=0, tiled=True)
        far = near
    else:
        near = exchange(outgoing)
        far = lax.ppermute(near, "exp", core_swap)
    keep, give, attended = experts(listing, near, far, attended, gate_weight, up_weight, down_weight)
    if RET16:
        returned = lax.all_to_all(give, "exp", split_axis=0, concat_axis=0, tiled=True)
    else:
        taken = lax.ppermute(give, "exp", core_swap)
        merged = pl.pallas_call(
            merge_kernel,
            out_shape=pltpu.VMEM((chips, CAP, width), jnp.bfloat16),
            in_specs=[vmem, vmem],
            out_specs=vmem,
            name="merge",
        )(in_vmem(keep), in_vmem(taken))
        returned = exchange(merged)
    expert_out = pl.pallas_call(
        combine_kernel,
        out_shape=jax.ShapeDtypeStruct(queries.shape, jnp.bfloat16),
        in_specs=[vmem, vmem],
        out_specs=vmem,
        name="combine",
    )(in_vmem(mix), in_vmem(returned))
    return attended, expert_out


def solution(mesh):
    rows = P(("dom", "exp"), None)
    return jax.shard_map(
        shards,
        mesh=mesh,
        in_specs=(
            rows,
            rows,
            rows,
            P(("dom", "exp"), None, None),
            P(("dom", "exp"), None, None),
            P(("dom", "exp")),
            P(),
            rows,
            rows,
            P("dom", None),
            P("exp", None),
            P("exp", None),
            P("exp", None),
        ),
        out_specs=(rows, rows),
        check_vma=False,
    )
```

```python
import math

import jax
import jax.numpy as jnp
from jax import lax
from jax.experimental import pallas as pl
from jax.experimental.pallas import tpu as pltpu
from jax.sharding import PartitionSpec as P

KV_HEADS = 8
BLOCK = 128
CAP = 2
EPSILON = 1e-05

QUAD = 4 * BLOCK
SLOTS = 8


vmem = pl.BlockSpec(memory_space=pltpu.VMEM)
smem = pl.BlockSpec(memory_space=pltpu.SMEM)
hbm = pl.BlockSpec(memory_space=pl.ANY)


def slot_of(ids_ref, row, choice):
    mine = ids_ref[choice, row]
    rank = jnp.int32(0)
    for r in range(row + 1):
        for k in range(2):
            if (r, k) < (row, choice):
                rank += (ids_ref[k, r] == mine).astype(jnp.int32)
    return mine * CAP + rank


def attend_kernel(
    lengths_ref,
    ids_ref,
    route_weights_ref,
    flags_ref,
    queries_ref,
    new_keys_ref,
    new_values_ref,
    keys_ref,
    values_ref,
    gain_ref,
    attended_ref,
    outgoing_ref,
    mix_ref,
    kept_gain_ref,
    list_ref,
):
    rows, width = queries_ref.shape
    context = keys_ref.shape[1]
    head_size = new_keys_ref.shape[1] // KV_HEADS
    group = width // head_size // KV_HEADS
    spots = rows * context
    stack = group * rows
    scale = head_size ** (-0.5)
    list_blocks(flags_ref, list_ref, list_ref.shape[1] - 1)
    query = queries_ref[...].astype(jnp.float32)
    new_key = new_keys_ref[...].astype(jnp.float32)
    new_value = new_values_ref[...].astype(jnp.float32)

    scores, owns = [], []
    for j in range(KV_HEADS):
        columns = slice(j * head_size, (j + 1) * head_size)
        heads = [query[:, (j * group + g) * head_size : (j * group + g + 1) * head_size] for g in range(group)]
        stacked = jnp.concatenate(heads, axis=0)
        keys = keys_ref[:, :, columns].reshape(spots, head_size)
        scores.append(
            lax.dot_general(
                stacked.astype(jnp.bfloat16), keys, (((1,), (1,)), ((), ())), preferred_element_type=jnp.float32
            )
        )
        own_key = jnp.concatenate([new_key[:, columns]] * group, axis=0)
        owns.append(jnp.sum(stacked * own_key, axis=1, keepdims=True))
    score = jnp.concatenate(scores, axis=0) * scale
    own = jnp.concatenate(owns, axis=0) * scale
    row_of_line = lax.broadcasted_iota(jnp.int32, score.shape, 0) % rows
    spot = lax.broadcasted_iota(jnp.int32, score.shape, 1)
    valid = jnp.zeros(score.shape, jnp.bool_)
    for r in range(rows):
        valid = valid | ((row_of_line == r) & (spot >= r * context) & (spot < r * context + lengths_ref[r]))
    score = jnp.where(valid, score, -jnp.inf)
    top = jnp.maximum(jnp.max(score, axis=1, keepdims=True), own)
    score_exp = jnp.exp(score - top)
    own_exp = jnp.exp(own - top)
    denominator = jnp.sum(score_exp, axis=1, keepdims=True) + own_exp
    prob = (score_exp / denominator).astype(jnp.bfloat16)
    own_prob = (own_exp / denominator).astype(jnp.bfloat16).astype(jnp.float32)

    pieces = []
    for j in range(KV_HEADS):
        columns = slice(j * head_size, (j + 1) * head_size)
        lines = slice(j * stack, (j + 1) * stack)
        values = values_ref[:, :, columns].reshape(spots, head_size)
        mixture = jnp.dot(prob[lines], values, preferred_element_type=jnp.float32)
        own_value = jnp.concatenate([new_value[:, columns]] * group, axis=0)
        mixture = mixture + own_prob[lines] * own_value
        pieces += [mixture[g * rows : (g + 1) * rows] for g in range(group)]
    attended = jnp.concatenate(pieces, axis=1).astype(jnp.bfloat16)
    attended_ref[...] = attended

    features = attended.astype(jnp.float32)
    places = outgoing_ref.shape[0]
    experts = flags_ref.shape[0]
    line = lax.broadcasted_iota(jnp.int32, (experts * CAP, 1), 0)
    mix_row = lax.broadcasted_iota(jnp.int32, mix_ref.shape, 0)
    mix_slot = lax.broadcasted_iota(jnp.int32, mix_ref.shape, 1)
    packed = jnp.zeros((experts * CAP, width), jnp.float32)
    mix = jnp.zeros(mix_ref.shape, jnp.float32)
    for r in range(rows):
        slots = [slot_of(ids_ref, r, k) for k in range(2)]
        packed = packed + jnp.where((line == slots[0]) | (line == slots[1]), features[r : r + 1, :], 0.0)
        for k in range(2):
            mix = mix + jnp.where((mix_row == r) & (mix_slot == slots[k]), route_weights_ref[k, r], 0.0)
    packed = packed.astype(jnp.bfloat16)
    for place in range(places):
        expert = place // (places // experts)
        outgoing_ref[place] = packed[expert * CAP : (expert + 1) * CAP, :]
    mix_ref[...] = mix
    kept_gain_ref[...] = gain_ref[...]


def list_blocks(flags_ref, list_ref, blocks):
    experts = flags_ref.shape[0]
    groups = lax.axis_size("exp") // experts
    position = lax.axis_index("exp")
    expert = position // groups
    first = (position % groups) * blocks

    count = jnp.int32(0)
    for b in range(blocks):
        list_ref[0, count] = b
        count += (flags_ref[expert, first + b] != 0).astype(jnp.int32)
    list_ref[0, blocks] = count


def item_copies(item, count, list_ref, weights, ring_ref, sems):
    gate_ref, up_ref, down_ref = weights
    pairs = (count + 1) // 2
    slot = item % ring_ref.shape[0]

    def copy(source_ref, position, part):
        rows = pl.ds(pl.multiple_of(list_ref[0, position] * BLOCK, BLOCK), BLOCK)
        return pltpu.make_async_copy(
            source_ref.at[rows, :], ring_ref.at[slot, pl.ds(part * BLOCK, BLOCK), :], sems.at[slot, part]
        )

    def apply(act):
        @pl.when(item < pairs)
        def _():
            for s in range(2):
                @pl.when(2 * item + s < count)
                def _():
                    act(copy(gate_ref, 2 * item + s, 2 * s))
                    act(copy(up_ref, 2 * item + s, 2 * s + 1))

        @pl.when(item >= pairs)
        def _():
            for s in range(2):
                position = 2 * (item - pairs) + s
                @pl.when(position < count)
                def _():
                    act(copy(down_ref, position, s))

    return apply


def experts_kernel(
    list_ref,
    near_ref,
    far_ref,
    attended_ref,
    gain_ref,
    gate_ref,
    up_ref,
    down_ref,
    keep_ref,
    give_ref,
    attended_out,
    ring_ref,
    x_ref,
    hidden_ref,
    total_ref,
    sems,
    attended_sem,
):
    blocks = gate_ref.shape[0] // BLOCK
    chips = x_ref.shape[0] // (2 * CAP)
    half = chips * CAP
    ring_slots = ring_ref.shape[0]
    count = list_ref[0, blocks]
    weights = (gate_ref, up_ref, down_ref)
    whole = count // 2
    pairs = (count + 1) // 2

    def start(item, carry):
        item_copies(item, count, list_ref, weights, ring_ref, sems)(lambda copy: copy.start())
        return carry

    def settle(item):
        item_copies(item, count, list_ref, weights, ring_ref, sems)(lambda copy: copy.wait())

    lax.fori_loop(0, ring_slots, start, 0)
    write = pltpu.make_async_copy(attended_ref, attended_out, attended_sem)
    write.start()
    for chip in range(chips):
        x_ref[chip * CAP : (chip + 1) * CAP, :] = near_ref[chip]
        x_ref[half + chip * CAP : half + (chip + 1) * CAP, :] = far_ref[chip]
    features = x_ref[...].astype(jnp.float32)
    mean_square = jnp.mean(features * features, axis=1, keepdims=True)
    features = features * lax.rsqrt(mean_square + EPSILON)
    x_ref[...] = (features * gain_ref[...]).astype(jnp.bfloat16)
    total_ref[...] = jnp.zeros_like(total_ref)

    def project(item, number):
        settle(item)
        slot = item % ring_slots
        both = lax.dot_general(
            ring_ref[slot, : 2 * number * BLOCK, :],
            x_ref[...],
            (((1,), (1,)), ((), ())),
            preferred_element_type=jnp.float32,
        )
        for s in range(number):
            gate = both[2 * s * BLOCK : (2 * s + 1) * BLOCK]
            up = both[(2 * s + 1) * BLOCK : (2 * s + 2) * BLOCK]
            hidden = (jax.nn.relu(gate) * jax.nn.relu(up)).T
            hidden_ref[item, :, s * BLOCK : (s + 1) * BLOCK] = hidden.astype(jnp.bfloat16)
        start(item + ring_slots, 0)

    def contract(chunk, number):
        item = pairs + chunk
        settle(item)
        total_ref[...] += jnp.dot(
            hidden_ref[chunk, :, : number * BLOCK],
            ring_ref[item % ring_slots, : number * BLOCK, :],
            preferred_element_type=jnp.float32,
        )
        start(item + ring_slots, 0)

    def steps(body):
        def pair(step, carry):
            body(step, 2)
            return carry

        lax.fori_loop(0, whole, pair, 0)

        @pl.when(whole < pairs)
        def _():
            body(whole, 1)

    steps(project)
    steps(contract)
    keep_ref[...] = total_ref[0:half, :]
    give_ref[...] = total_ref[half:, :].astype(jnp.bfloat16)
    write.wait()


def merge_kernel(keep_ref, taken_ref, out_ref):
    total = (keep_ref[...] + taken_ref[...].astype(jnp.float32)).astype(jnp.bfloat16)
    for chip in range(out_ref.shape[0]):
        out_ref[chip] = total[chip * CAP : (chip + 1) * CAP, :]


def combine_kernel(mix_ref, returned_ref, out_ref):
    rows = out_ref.shape[0]
    experts = mix_ref.shape[1] // CAP
    share = returned_ref.shape[0] // experts
    mix = mix_ref[...]
    high = mix.astype(jnp.bfloat16)
    rest = mix - high.astype(jnp.float32)
    middle = rest.astype(jnp.bfloat16)
    low = (rest - middle.astype(jnp.float32)).astype(jnp.bfloat16)
    weights = jnp.concatenate([high] * share + [middle] * share + [low] * share, axis=1)
    parts = [
        returned_ref[expert * share + part] for part in range(share) for expert in range(experts)
    ]
    values = jnp.concatenate(parts * 3, axis=0)
    total = jnp.dot(weights, values, preferred_element_type=jnp.float32)
    out_ref[...] = total[0:rows].astype(jnp.bfloat16)


def ring_of(gate_weight):
    blocks, width = gate_weight.shape[0] // BLOCK, gate_weight.shape[1]
    slots = min(SLOTS, (blocks + 1) // 2 * 2)
    return blocks, (slots, QUAD, width)


def in_vmem(array):
    return pltpu.with_memory_space_constraint(array, pltpu.VMEM)


def experts(listing, near, far, attended, gain, gate_weight, up_weight, down_weight):
    blocks, ring_shape = ring_of(gate_weight)
    half, width = near.shape[0] * CAP, near.shape[2]
    return pl.pallas_call(
        experts_kernel,
        out_shape=(
            pltpu.VMEM((half, width), jnp.float32),
            pltpu.VMEM((half, width), jnp.bfloat16),
            jax.ShapeDtypeStruct(attended.shape, jnp.bfloat16),
        ),
        in_specs=[smem] + [vmem] * 4 + [hbm] * 3,
        out_specs=(vmem, vmem, hbm),
        scratch_shapes=[
            pltpu.VMEM(ring_shape, jnp.bfloat16),
            pltpu.VMEM((2 * half, width), jnp.bfloat16),
            pltpu.VMEM(((blocks + 1) // 2, 2 * half, 2 * BLOCK), jnp.bfloat16),
            pltpu.VMEM((2 * half, width), jnp.float32),
            pltpu.SemaphoreType.DMA((ring_shape[0], 4)),
            pltpu.SemaphoreType.DMA,
        ],
        compiler_params=pltpu.CompilerParams(vmem_limit_bytes=6 * 2**20 + 16 * half * width + 2 * math.prod(ring_shape)),
        name="experts",
    )(
        pltpu.with_memory_space_constraint(listing, pltpu.SMEM),
        in_vmem(near),
        in_vmem(far),
        in_vmem(attended),
        in_vmem(gain),
        *(pltpu.with_memory_space_constraint(weight, pltpu.HBM) for weight in (gate_weight, up_weight, down_weight)),
    )


def shards(
    queries,
    new_keys,
    new_values,
    cache_keys,
    cache_values,
    lengths,
    norm_gain,
    route_ids,
    route_weights,
    active_blocks,
    gate_weight,
    up_weight,
    down_weight,
):
    devices = lax.axis_size("exp")
    chips = devices // 2
    width = queries.shape[1]
    half = chips * CAP
    same_core = [[2 * chip + core for chip in range(chips)] for core in range(2)]
    core_swap = [(device, device ^ 1) for device in range(devices)]

    experts_number = active_blocks.shape[0]
    attended, outgoing, mix, gain, listing = pl.pallas_call(
        attend_kernel,
        out_shape=(
            pltpu.VMEM(queries.shape, jnp.bfloat16),
            pltpu.VMEM((chips, CAP, width), jnp.bfloat16),
            pltpu.VMEM((8, experts_number * CAP), jnp.float32),
            pltpu.VMEM((1, width), jnp.float32),
            pltpu.SMEM((1, gate_weight.shape[0] // BLOCK + 1), jnp.int32),
        ),
        in_specs=[smem] * 4 + [vmem] * 6,
        out_specs=(vmem, vmem, vmem, vmem, smem),
        name="attend",
    )(
        lengths,
        route_ids.T,
        route_weights.T,
        active_blocks,
        queries,
        new_keys,
        new_values,
        cache_keys,
        cache_values,
        norm_gain[None, :],
    )

    def exchange(array):
        return lax.all_to_all(array, "exp", split_axis=0, concat_axis=0, tiled=True, axis_index_groups=same_core)

    near = exchange(outgoing)
    far = lax.ppermute(near, "exp", core_swap)
    keep, give, attended = experts(listing, near, far, attended, gain, gate_weight, up_weight, down_weight)
    taken = lax.ppermute(give, "exp", core_swap)
    merged = pl.pallas_call(
        merge_kernel,
        out_shape=pltpu.VMEM((chips, CAP, width), jnp.bfloat16),
        in_specs=[vmem, vmem],
        out_specs=vmem,
        name="merge",
    )(in_vmem(keep), in_vmem(taken))
    returned = exchange(merged)
    expert_out = pl.pallas_call(
        combine_kernel,
        out_shape=jax.ShapeDtypeStruct(queries.shape, jnp.bfloat16),
        in_specs=[vmem, vmem],
        out_specs=vmem,
        name="combine",
    )(in_vmem(mix), in_vmem(returned))
    return attended, expert_out


def solution(mesh):
    rows = P(("dom", "exp"), None)
    return jax.shard_map(
        shards,
        mesh=mesh,
        in_specs=(
            rows,
            rows,
            rows,
            P(("dom", "exp"), None, None),
            P(("dom", "exp"), None, None),
            P(("dom", "exp")),
            P(),
            rows,
            rows,
            P("dom", None),
            P("exp", None),
            P("exp", None),
            P("exp", None),
        ),
        out_specs=(rows, rows),
        check_vma=False,
    )
```

```python
import math

import jax
import jax.numpy as jnp
from jax import lax
from jax.experimental import pallas as pl
from jax.experimental.pallas import tpu as pltpu
from jax.sharding import PartitionSpec as P

KV_HEADS = 8
BLOCK = 128
CAP = 2
EPSILON = 1e-05

QUAD = 4 * BLOCK
SLOTS = 8


vmem = pl.BlockSpec(memory_space=pltpu.VMEM)
smem = pl.BlockSpec(memory_space=pltpu.SMEM)
hbm = pl.BlockSpec(memory_space=pl.ANY)


def slot_of(ids_ref, row, choice):
    mine = ids_ref[choice, row]
    rank = jnp.int32(0)
    for r in range(row + 1):
        for k in range(2):
            if (r, k) < (row, choice):
                rank += (ids_ref[k, r] == mine).astype(jnp.int32)
    return mine * CAP + rank


def attend_kernel(
    lengths_ref,
    ids_ref,
    route_weights_ref,
    flags_ref,
    queries_ref,
    new_keys_ref,
    new_values_ref,
    keys_ref,
    values_ref,
    gain_ref,
    attended_ref,
    outgoing_ref,
    mix_ref,
    kept_gain_ref,
    list_ref,
):
    rows, width = queries_ref.shape
    context = keys_ref.shape[1]
    head_size = new_keys_ref.shape[1] // KV_HEADS
    group = width // head_size // KV_HEADS
    spots = rows * context
    stack = group * rows
    scale = head_size ** (-0.5)
    list_blocks(flags_ref, list_ref, list_ref.shape[1] - 1)
    query = queries_ref[...].astype(jnp.float32)
    new_key = new_keys_ref[...].astype(jnp.float32)
    new_value = new_values_ref[...].astype(jnp.float32)

    scores, owns = [], []
    for j in range(KV_HEADS):
        columns = slice(j * head_size, (j + 1) * head_size)
        heads = [query[:, (j * group + g) * head_size : (j * group + g + 1) * head_size] for g in range(group)]
        stacked = jnp.concatenate(heads, axis=0)
        keys = keys_ref[:, :, columns].reshape(spots, head_size)
        scores.append(
            lax.dot_general(
                stacked.astype(jnp.bfloat16), keys, (((1,), (1,)), ((), ())), preferred_element_type=jnp.float32
            )
        )
        own_key = jnp.concatenate([new_key[:, columns]] * group, axis=0)
        owns.append(jnp.sum(stacked * own_key, axis=1, keepdims=True))
    score = jnp.concatenate(scores, axis=0) * scale
    own = jnp.concatenate(owns, axis=0) * scale
    row_of_line = lax.broadcasted_iota(jnp.int32, score.shape, 0) % rows
    spot = lax.broadcasted_iota(jnp.int32, score.shape, 1)
    valid = jnp.zeros(score.shape, jnp.bool_)
    for r in range(rows):
        valid = valid | ((row_of_line == r) & (spot >= r * context) & (spot < r * context + lengths_ref[r]))
    score = jnp.where(valid, score, -jnp.inf)
    top = jnp.maximum(jnp.max(score, axis=1, keepdims=True), own)
    score_exp = jnp.exp(score - top)
    own_exp = jnp.exp(own - top)
    denominator = jnp.sum(score_exp, axis=1, keepdims=True) + own_exp
    prob = (score_exp / denominator).astype(jnp.bfloat16)
    own_prob = (own_exp / denominator).astype(jnp.bfloat16).astype(jnp.float32)

    pieces = []
    for j in range(KV_HEADS):
        columns = slice(j * head_size, (j + 1) * head_size)
        lines = slice(j * stack, (j + 1) * stack)
        values = values_ref[:, :, columns].reshape(spots, head_size)
        mixture = jnp.dot(prob[lines], values, preferred_element_type=jnp.float32)
        own_value = jnp.concatenate([new_value[:, columns]] * group, axis=0)
        mixture = mixture + own_prob[lines] * own_value
        pieces += [mixture[g * rows : (g + 1) * rows] for g in range(group)]
    attended = jnp.concatenate(pieces, axis=1).astype(jnp.bfloat16)
    attended_ref[...] = attended

    features = attended.astype(jnp.float32)
    places = outgoing_ref.shape[0]
    experts = flags_ref.shape[0]
    line = lax.broadcasted_iota(jnp.int32, (experts * CAP, 1), 0)
    mix_row = lax.broadcasted_iota(jnp.int32, mix_ref.shape, 0)
    mix_slot = lax.broadcasted_iota(jnp.int32, mix_ref.shape, 1)
    packed = jnp.zeros((experts * CAP, width), jnp.float32)
    mix = jnp.zeros(mix_ref.shape, jnp.float32)
    for r in range(rows):
        slots = [slot_of(ids_ref, r, k) for k in range(2)]
        packed = packed + jnp.where((line == slots[0]) | (line == slots[1]), features[r : r + 1, :], 0.0)
        for k in range(2):
            mix = mix + jnp.where((mix_row == r) & (mix_slot == slots[k]), route_weights_ref[k, r], 0.0)
    packed = packed.astype(jnp.bfloat16)
    for place in range(places):
        expert = place // (places // experts)
        outgoing_ref[place] = packed[expert * CAP : (expert + 1) * CAP, :]
    mix_ref[...] = mix
    kept_gain_ref[...] = gain_ref[...]


def list_blocks(flags_ref, list_ref, blocks):
    experts = flags_ref.shape[0]
    groups = lax.axis_size("exp") // experts
    position = lax.axis_index("exp")
    expert = position // groups
    first = (position % groups) * blocks

    count = jnp.int32(0)
    for b in range(blocks):
        list_ref[0, count] = b
        count += (flags_ref[expert, first + b] != 0).astype(jnp.int32)
    list_ref[0, blocks] = count


def item_copies(item, count, list_ref, weights, ring_ref, sems):
    gate_ref, up_ref, down_ref = weights
    pairs = (count + 1) // 2
    slot = item % ring_ref.shape[0]

    def copy(source_ref, position, part):
        rows = pl.ds(pl.multiple_of(list_ref[0, position] * BLOCK, BLOCK), BLOCK)
        return pltpu.make_async_copy(
            source_ref.at[rows, :], ring_ref.at[slot, pl.ds(part * BLOCK, BLOCK), :], sems.at[slot, part]
        )

    def apply(act):
        @pl.when(item < pairs)
        def _():
            for s in range(2):
                @pl.when(2 * item + s < count)
                def _():
                    act(copy(gate_ref, 2 * item + s, 2 * s))
                    act(copy(up_ref, 2 * item + s, 2 * s + 1))

        @pl.when(item >= pairs)
        def _():
            for s in range(2):
                position = 2 * (item - pairs) + s
                @pl.when(position < count)
                def _():
                    act(copy(down_ref, position, s))

    return apply


def experts_kernel(
    list_ref,
    near_ref,
    far_ref,
    attended_ref,
    gain_ref,
    gate_ref,
    up_ref,
    down_ref,
    keep_ref,
    give_ref,
    attended_out,
    ring_ref,
    x_ref,
    hidden_ref,
    total_ref,
    sems,
    attended_sem,
):
    blocks = gate_ref.shape[0] // BLOCK
    chips = x_ref.shape[0] // (2 * CAP)
    half = chips * CAP
    ring_slots = ring_ref.shape[0]
    count = list_ref[0, blocks]
    weights = (gate_ref, up_ref, down_ref)
    whole = count // 2
    pairs = (count + 1) // 2

    def start(item, carry):
        item_copies(item, count, list_ref, weights, ring_ref, sems)(lambda copy: copy.start())
        return carry

    def settle(item):
        item_copies(item, count, list_ref, weights, ring_ref, sems)(lambda copy: copy.wait())

    lax.fori_loop(0, ring_slots, start, 0)
    write = pltpu.make_async_copy(attended_ref, attended_out, attended_sem)
    write.start()
    for chip in range(chips):
        x_ref[chip * CAP : (chip + 1) * CAP, :] = near_ref[chip]
        x_ref[half + chip * CAP : half + (chip + 1) * CAP, :] = far_ref[chip]
    features = x_ref[...].astype(jnp.float32)
    mean_square = jnp.mean(features * features, axis=1, keepdims=True)
    features = features * lax.rsqrt(mean_square + EPSILON)
    x_ref[...] = (features * gain_ref[...]).astype(jnp.bfloat16)
    total_ref[...] = jnp.zeros_like(total_ref)

    def project(item, number):
        settle(item)
        slot = item % ring_slots
        both = lax.dot_general(
            ring_ref[slot, : 2 * number * BLOCK, :],
            x_ref[...],
            (((1,), (1,)), ((), ())),
            preferred_element_type=jnp.float32,
        )
        for s in range(number):
            gate = both[2 * s * BLOCK : (2 * s + 1) * BLOCK]
            up = both[(2 * s + 1) * BLOCK : (2 * s + 2) * BLOCK]
            hidden = (jax.nn.relu(gate) * jax.nn.relu(up)).T
            hidden_ref[item, :, s * BLOCK : (s + 1) * BLOCK] = hidden.astype(jnp.bfloat16)
        start(item + ring_slots, 0)

    def contract(chunk, blocks_of):
        items = [pairs + chunk + i for i in range(len(blocks_of))]
        for item in items:
            settle(item)
        products = [
            jnp.dot(
                hidden_ref[chunk + i, :, : number * BLOCK],
                ring_ref[items[i] % ring_slots, : number * BLOCK, :],
                preferred_element_type=jnp.float32,
            )
            for i, number in enumerate(blocks_of)
        ]
        total_ref[...] += sum(products[1:], products[0])
        for item in items:
            start(item + ring_slots, 0)

    def project_pair(item, carry):
        project(item, 2)
        return carry

    def contract_wide(step, carry):
        contract(2 * step, (2,) * 2)
        return carry

    def contract_pair(chunk, carry):
        contract(chunk, (2,))
        return carry

    lax.fori_loop(0, whole, project_pair, 0)

    @pl.when(whole < pairs)
    def _():
        project(whole, 1)

    wide = jnp.maximum(whole - 1, 0) // 2
    lax.fori_loop(0, wide, contract_wide, 0)
    lax.fori_loop(2 * wide, whole, contract_pair, 0)

    @pl.when(whole < pairs)
    def _():
        contract(whole, (1,))

    keep_ref[...] = total_ref[0:half, :]
    give_ref[...] = total_ref[half:, :].astype(jnp.bfloat16)
    write.wait()


def merge_kernel(keep_ref, taken_ref, out_ref):
    total = (keep_ref[...] + taken_ref[...].astype(jnp.float32)).astype(jnp.bfloat16)
    for chip in range(out_ref.shape[0]):
        out_ref[chip] = total[chip * CAP : (chip + 1) * CAP, :]


def combine_kernel(mix_ref, returned_ref, out_ref):
    rows = out_ref.shape[0]
    experts = mix_ref.shape[1] // CAP
    share = returned_ref.shape[0] // experts
    mix = mix_ref[...]
    high = mix.astype(jnp.bfloat16)
    rest = mix - high.astype(jnp.float32)
    middle = rest.astype(jnp.bfloat16)
    low = (rest - middle.astype(jnp.float32)).astype(jnp.bfloat16)
    weights = jnp.concatenate([high] * share + [middle] * share + [low] * share, axis=1)
    parts = [
        returned_ref[expert * share + part] for part in range(share) for expert in range(experts)
    ]
    values = jnp.concatenate(parts * 3, axis=0)
    total = jnp.dot(weights, values, preferred_element_type=jnp.float32)
    out_ref[...] = total[0:rows].astype(jnp.bfloat16)


def ring_of(gate_weight):
    blocks, width = gate_weight.shape[0] // BLOCK, gate_weight.shape[1]
    slots = min(SLOTS, (blocks + 1) // 2 * 2)
    return blocks, (slots, QUAD, width)


def in_vmem(array):
    return pltpu.with_memory_space_constraint(array, pltpu.VMEM)


def experts(listing, near, far, attended, gain, gate_weight, up_weight, down_weight):
    blocks, ring_shape = ring_of(gate_weight)
    half, width = near.shape[0] * CAP, near.shape[2]
    return pl.pallas_call(
        experts_kernel,
        out_shape=(
            pltpu.VMEM((half, width), jnp.float32),
            pltpu.VMEM((half, width), jnp.bfloat16),
            jax.ShapeDtypeStruct(attended.shape, jnp.bfloat16),
        ),
        in_specs=[smem] + [vmem] * 4 + [hbm] * 3,
        out_specs=(vmem, vmem, hbm),
        scratch_shapes=[
            pltpu.VMEM(ring_shape, jnp.bfloat16),
            pltpu.VMEM((2 * half, width), jnp.bfloat16),
            pltpu.VMEM(((blocks + 1) // 2, 2 * half, 2 * BLOCK), jnp.bfloat16),
            pltpu.VMEM((2 * half, width), jnp.float32),
            pltpu.SemaphoreType.DMA((ring_shape[0], 4)),
            pltpu.SemaphoreType.DMA,
        ],
        compiler_params=pltpu.CompilerParams(vmem_limit_bytes=6 * 2**20 + 16 * half * width + 2 * math.prod(ring_shape)),
        name="experts",
    )(
        pltpu.with_memory_space_constraint(listing, pltpu.SMEM),
        in_vmem(near),
        in_vmem(far),
        in_vmem(attended),
        in_vmem(gain),
        *(pltpu.with_memory_space_constraint(weight, pltpu.HBM) for weight in (gate_weight, up_weight, down_weight)),
    )


def shards(
    queries,
    new_keys,
    new_values,
    cache_keys,
    cache_values,
    lengths,
    norm_gain,
    route_ids,
    route_weights,
    active_blocks,
    gate_weight,
    up_weight,
    down_weight,
):
    devices = lax.axis_size("exp")
    chips = devices // 2
    width = queries.shape[1]
    half = chips * CAP
    same_core = [[2 * chip + core for chip in range(chips)] for core in range(2)]
    core_swap = [(device, device ^ 1) for device in range(devices)]

    experts_number = active_blocks.shape[0]
    attended, outgoing, mix, gain, listing = pl.pallas_call(
        attend_kernel,
        out_shape=(
            pltpu.VMEM(queries.shape, jnp.bfloat16),
            pltpu.VMEM((chips, CAP, width), jnp.bfloat16),
            pltpu.VMEM((8, experts_number * CAP), jnp.float32),
            pltpu.VMEM((1, width), jnp.float32),
            pltpu.SMEM((1, gate_weight.shape[0] // BLOCK + 1), jnp.int32),
        ),
        in_specs=[smem] * 4 + [vmem] * 6,
        out_specs=(vmem, vmem, vmem, vmem, smem),
        name="attend",
    )(
        lengths,
        route_ids.T,
        route_weights.T,
        active_blocks,
        queries,
        new_keys,
        new_values,
        cache_keys,
        cache_values,
        norm_gain[None, :],
    )

    def exchange(array):
        return lax.all_to_all(array, "exp", split_axis=0, concat_axis=0, tiled=True, axis_index_groups=same_core)

    near = exchange(outgoing)
    far = lax.ppermute(near, "exp", core_swap)
    keep, give, attended = experts(listing, near, far, attended, gain, gate_weight, up_weight, down_weight)
    taken = lax.ppermute(give, "exp", core_swap)
    merged = pl.pallas_call(
        merge_kernel,
        out_shape=pltpu.VMEM((chips, CAP, width), jnp.bfloat16),
        in_specs=[vmem, vmem],
        out_specs=vmem,
        name="merge",
    )(in_vmem(keep), in_vmem(taken))
    returned = exchange(merged)
    expert_out = pl.pallas_call(
        combine_kernel,
        out_shape=jax.ShapeDtypeStruct(queries.shape, jnp.bfloat16),
        in_specs=[vmem, vmem],
        out_specs=vmem,
        name="combine",
    )(in_vmem(mix), in_vmem(returned))
    return attended, expert_out


def solution(mesh):
    rows = P(("dom", "exp"), None)
    return jax.shard_map(
        shards,
        mesh=mesh,
        in_specs=(
            rows,
            rows,
            rows,
            P(("dom", "exp"), None, None),
            P(("dom", "exp"), None, None),
            P(("dom", "exp")),
            P(),
            rows,
            rows,
            P("dom", None),
            P("exp", None),
            P("exp", None),
            P("exp", None),
        ),
        out_specs=(rows, rows),
        check_vma=False,
    )
```

```python
import math

import jax
import jax.numpy as jnp
from jax import lax
from jax.experimental import pallas as pl
from jax.experimental.pallas import tpu as pltpu
from jax.sharding import PartitionSpec as P

KV_HEADS = 8
BLOCK = 128
CAP = 2
EPSILON = 1e-05

QUAD = 4 * BLOCK
SLOTS = 7


vmem = pl.BlockSpec(memory_space=pltpu.VMEM)
smem = pl.BlockSpec(memory_space=pltpu.SMEM)
hbm = pl.BlockSpec(memory_space=pl.ANY)


def slot_of(ids_ref, row, choice):
    mine = ids_ref[choice, row]
    rank = jnp.int32(0)
    for r in range(row + 1):
        for k in range(2):
            if (r, k) < (row, choice):
                rank += (ids_ref[k, r] == mine).astype(jnp.int32)
    return mine * CAP + rank


def attend_kernel(
    lengths_ref,
    ids_ref,
    route_weights_ref,
    flags_ref,
    queries_ref,
    new_keys_ref,
    new_values_ref,
    keys_ref,
    values_ref,
    gain_ref,
    attended_ref,
    outgoing_ref,
    mix_ref,
    kept_gain_ref,
    list_ref,
):
    rows, width = queries_ref.shape
    context = keys_ref.shape[1]
    head_size = new_keys_ref.shape[1] // KV_HEADS
    group = width // head_size // KV_HEADS
    spots = rows * context
    stack = group * rows
    scale = head_size ** (-0.5)
    list_blocks(flags_ref, list_ref, list_ref.shape[1] - 1)
    query = queries_ref[...].astype(jnp.float32)
    new_key = new_keys_ref[...].astype(jnp.float32)
    new_value = new_values_ref[...].astype(jnp.float32)

    scores, owns = [], []
    for j in range(KV_HEADS):
        columns = slice(j * head_size, (j + 1) * head_size)
        heads = [query[:, (j * group + g) * head_size : (j * group + g + 1) * head_size] for g in range(group)]
        stacked = jnp.concatenate(heads, axis=0)
        keys = keys_ref[:, :, columns].reshape(spots, head_size)
        scores.append(
            lax.dot_general(
                stacked.astype(jnp.bfloat16), keys, (((1,), (1,)), ((), ())), preferred_element_type=jnp.float32
            )
        )
        own_key = jnp.concatenate([new_key[:, columns]] * group, axis=0)
        owns.append(jnp.sum(stacked * own_key, axis=1, keepdims=True))
    score = jnp.concatenate(scores, axis=0) * scale
    own = jnp.concatenate(owns, axis=0) * scale
    row_of_line = lax.broadcasted_iota(jnp.int32, score.shape, 0) % rows
    spot = lax.broadcasted_iota(jnp.int32, score.shape, 1)
    valid = jnp.zeros(score.shape, jnp.bool_)
    for r in range(rows):
        valid = valid | ((row_of_line == r) & (spot >= r * context) & (spot < r * context + lengths_ref[r]))
    score = jnp.where(valid, score, -jnp.inf)
    top = jnp.maximum(jnp.max(score, axis=1, keepdims=True), own)
    score_exp = jnp.exp(score - top)
    own_exp = jnp.exp(own - top)
    denominator = jnp.sum(score_exp, axis=1, keepdims=True) + own_exp
    prob = (score_exp / denominator).astype(jnp.bfloat16)
    own_prob = (own_exp / denominator).astype(jnp.bfloat16).astype(jnp.float32)

    pieces = []
    for j in range(KV_HEADS):
        columns = slice(j * head_size, (j + 1) * head_size)
        lines = slice(j * stack, (j + 1) * stack)
        values = values_ref[:, :, columns].reshape(spots, head_size)
        mixture = jnp.dot(prob[lines], values, preferred_element_type=jnp.float32)
        own_value = jnp.concatenate([new_value[:, columns]] * group, axis=0)
        mixture = mixture + own_prob[lines] * own_value
        pieces += [mixture[g * rows : (g + 1) * rows] for g in range(group)]
    attended = jnp.concatenate(pieces, axis=1).astype(jnp.bfloat16)
    attended_ref[...] = attended

    features = attended.astype(jnp.float32)
    places = outgoing_ref.shape[0]
    experts = flags_ref.shape[0]
    line = lax.broadcasted_iota(jnp.int32, (experts * CAP, 1), 0)
    mix_row = lax.broadcasted_iota(jnp.int32, mix_ref.shape, 0)
    mix_slot = lax.broadcasted_iota(jnp.int32, mix_ref.shape, 1)
    packed = jnp.zeros((experts * CAP, width), jnp.float32)
    mix = jnp.zeros(mix_ref.shape, jnp.float32)
    for r in range(rows):
        slots = [slot_of(ids_ref, r, k) for k in range(2)]
        packed = packed + jnp.where((line == slots[0]) | (line == slots[1]), features[r : r + 1, :], 0.0)
        for k in range(2):
            mix = mix + jnp.where((mix_row == r) & (mix_slot == slots[k]), route_weights_ref[k, r], 0.0)
    packed = packed.astype(jnp.bfloat16)
    for place in range(places):
        expert = place // (places // experts)
        outgoing_ref[place] = packed[expert * CAP : (expert + 1) * CAP, :]
    mix_ref[...] = mix
    kept_gain_ref[...] = gain_ref[...]


def list_blocks(flags_ref, list_ref, blocks):
    experts = flags_ref.shape[0]
    groups = lax.axis_size("exp") // experts
    position = lax.axis_index("exp")
    expert = position // groups
    first = (position % groups) * blocks

    count = jnp.int32(0)
    for b in range(blocks):
        list_ref[0, count] = b
        count += (flags_ref[expert, first + b] != 0).astype(jnp.int32)
    list_ref[0, blocks] = count


def item_copies(item, count, list_ref, weights, ring_ref, sems):
    gate_ref, up_ref, down_ref = weights
    pairs = (count + 1) // 2
    slot = item % ring_ref.shape[0]

    def copy(source_ref, position, part):
        rows = pl.ds(pl.multiple_of(list_ref[0, position] * BLOCK, BLOCK), BLOCK)
        return pltpu.make_async_copy(
            source_ref.at[rows, :], ring_ref.at[slot, pl.ds(part * BLOCK, BLOCK), :], sems.at[slot, part]
        )

    def apply(act):
        @pl.when(item < pairs)
        def _():
            for s in range(2):
                @pl.when(2 * item + s < count)
                def _():
                    act(copy(gate_ref, 2 * item + s, 2 * s))
                    act(copy(up_ref, 2 * item + s, 2 * s + 1))

        @pl.when(item >= pairs)
        def _():
            for s in range(2):
                position = 2 * (item - pairs) + s
                @pl.when(position < count)
                def _():
                    act(copy(down_ref, position, s))

    return apply


def experts_kernel(
    list_ref,
    near_ref,
    far_ref,
    attended_ref,
    gain_ref,
    gate_ref,
    up_ref,
    down_ref,
    keep_ref,
    give_ref,
    attended_out,
    ring_ref,
    x_ref,
    hidden_ref,
    total_ref,
    sems,
    attended_sem,
):
    blocks = gate_ref.shape[0] // BLOCK
    chips = x_ref.shape[0] // (2 * CAP)
    half = chips * CAP
    ring_slots = ring_ref.shape[0]
    count = list_ref[0, blocks]
    weights = (gate_ref, up_ref, down_ref)
    whole = count // 2
    pairs = (count + 1) // 2

    def start(item, carry):
        item_copies(item, count, list_ref, weights, ring_ref, sems)(lambda copy: copy.start())
        return carry

    def settle(item):
        item_copies(item, count, list_ref, weights, ring_ref, sems)(lambda copy: copy.wait())

    lax.fori_loop(0, ring_slots, start, 0)
    write = pltpu.make_async_copy(attended_ref, attended_out, attended_sem)
    write.start()
    for chip in range(chips):
        x_ref[chip * CAP : (chip + 1) * CAP, :] = near_ref[chip]
        x_ref[half + chip * CAP : half + (chip + 1) * CAP, :] = far_ref[chip]
    features = x_ref[...].astype(jnp.float32)
    mean_square = jnp.mean(features * features, axis=1, keepdims=True)
    features = features * lax.rsqrt(mean_square + EPSILON)
    x_ref[...] = (features * gain_ref[...]).astype(jnp.bfloat16)
    total_ref[...] = jnp.zeros_like(total_ref)

    def project(item, number):
        settle(item)
        slot = item % ring_slots
        both = lax.dot_general(
            ring_ref[slot, : 2 * number * BLOCK, :],
            x_ref[...],
            (((1,), (1,)), ((), ())),
            preferred_element_type=jnp.float32,
        )
        for s in range(number):
            gate = both[2 * s * BLOCK : (2 * s + 1) * BLOCK]
            up = both[(2 * s + 1) * BLOCK : (2 * s + 2) * BLOCK]
            hidden = (jax.nn.relu(gate) * jax.nn.relu(up)).T
            hidden_ref[item, :, s * BLOCK : (s + 1) * BLOCK] = hidden.astype(jnp.bfloat16)
        start(item + ring_slots, 0)

    def contract(chunk, number):
        item = pairs + chunk
        settle(item)
        total_ref[...] += jnp.dot(
            hidden_ref[chunk, :, : number * BLOCK],
            ring_ref[item % ring_slots, : number * BLOCK, :],
            preferred_element_type=jnp.float32,
        )
        start(item + ring_slots, 0)

    def steps(body):
        def pair(step, carry):
            body(step, 2)
            return carry

        lax.fori_loop(0, whole, pair, 0)

        @pl.when(whole < pairs)
        def _():
            body(whole, 1)

    steps(project)
    steps(contract)
    keep_ref[...] = total_ref[0:half, :]
    give_ref[...] = total_ref[half:, :].astype(jnp.bfloat16)
    write.wait()


def merge_kernel(keep_ref, taken_ref, out_ref):
    total = (keep_ref[...] + taken_ref[...].astype(jnp.float32)).astype(jnp.bfloat16)
    for chip in range(out_ref.shape[0]):
        out_ref[chip] = total[chip * CAP : (chip + 1) * CAP, :]


def combine_kernel(mix_ref, returned_ref, out_ref):
    rows = out_ref.shape[0]
    experts = mix_ref.shape[1] // CAP
    share = returned_ref.shape[0] // experts
    mix = mix_ref[...]
    high = mix.astype(jnp.bfloat16)
    rest = mix - high.astype(jnp.float32)
    middle = rest.astype(jnp.bfloat16)
    low = (rest - middle.astype(jnp.float32)).astype(jnp.bfloat16)
    weights = jnp.concatenate([high] * share + [middle] * share + [low] * share, axis=1)
    parts = [
        returned_ref[expert * share + part] for part in range(share) for expert in range(experts)
    ]
    values = jnp.concatenate(parts * 3, axis=0)
    total = jnp.dot(weights, values, preferred_element_type=jnp.float32)
    out_ref[...] = total[0:rows].astype(jnp.bfloat16)


def ring_of(gate_weight):
    blocks, width = gate_weight.shape[0] // BLOCK, gate_weight.shape[1]
    slots = min(SLOTS, (blocks + 1) // 2 * 2)
    return blocks, (slots, QUAD, width)


def in_vmem(array):
    return pltpu.with_memory_space_constraint(array, pltpu.VMEM)


def experts(listing, near, far, attended, gain, gate_weight, up_weight, down_weight):
    blocks, ring_shape = ring_of(gate_weight)
    half, width = near.shape[0] * CAP, near.shape[2]
    return pl.pallas_call(
        experts_kernel,
        out_shape=(
            pltpu.VMEM((half, width), jnp.float32),
            pltpu.VMEM((half, width), jnp.bfloat16),
            jax.ShapeDtypeStruct(attended.shape, jnp.bfloat16),
        ),
        in_specs=[smem] + [vmem] * 4 + [hbm] * 3,
        out_specs=(vmem, vmem, hbm),
        scratch_shapes=[
            pltpu.VMEM(ring_shape, jnp.bfloat16),
            pltpu.VMEM((2 * half, width), jnp.bfloat16),
            pltpu.VMEM(((blocks + 1) // 2, 2 * half, 2 * BLOCK), jnp.bfloat16),
            pltpu.VMEM((2 * half, width), jnp.float32),
            pltpu.SemaphoreType.DMA((ring_shape[0], 4)),
            pltpu.SemaphoreType.DMA,
        ],
        compiler_params=pltpu.CompilerParams(vmem_limit_bytes=6 * 2**20 + 16 * half * width + 2 * math.prod(ring_shape)),
        name="experts",
    )(
        pltpu.with_memory_space_constraint(listing, pltpu.SMEM),
        in_vmem(near),
        in_vmem(far),
        in_vmem(attended),
        in_vmem(gain),
        *(pltpu.with_memory_space_constraint(weight, pltpu.HBM) for weight in (gate_weight, up_weight, down_weight)),
    )


def shards(
    queries,
    new_keys,
    new_values,
    cache_keys,
    cache_values,
    lengths,
    norm_gain,
    route_ids,
    route_weights,
    active_blocks,
    gate_weight,
    up_weight,
    down_weight,
):
    devices = lax.axis_size("exp")
    chips = devices // 2
    width = queries.shape[1]
    half = chips * CAP
    same_core = [[2 * chip + core for chip in range(chips)] for core in range(2)]
    core_swap = [(device, device ^ 1) for device in range(devices)]

    experts_number = active_blocks.shape[0]
    attended, outgoing, mix, gain, listing = pl.pallas_call(
        attend_kernel,
        out_shape=(
            pltpu.VMEM(queries.shape, jnp.bfloat16),
            pltpu.VMEM((chips, CAP, width), jnp.bfloat16),
            pltpu.VMEM((8, experts_number * CAP), jnp.float32),
            pltpu.VMEM((1, width), jnp.float32),
            pltpu.SMEM((1, gate_weight.shape[0] // BLOCK + 1), jnp.int32),
        ),
        in_specs=[smem] * 4 + [vmem] * 6,
        out_specs=(vmem, vmem, vmem, vmem, smem),
        name="attend",
    )(
        lengths,
        route_ids.T,
        route_weights.T,
        active_blocks,
        queries,
        new_keys,
        new_values,
        cache_keys,
        cache_values,
        norm_gain[None, :],
    )

    def exchange(array):
        return lax.all_to_all(array, "exp", split_axis=0, concat_axis=0, tiled=True, axis_index_groups=same_core)

    near = exchange(outgoing)
    far = lax.ppermute(near, "exp", core_swap)
    keep, give, attended = experts(listing, near, far, attended, gain, gate_weight, up_weight, down_weight)
    taken = lax.ppermute(give, "exp", core_swap)
    merged = pl.pallas_call(
        merge_kernel,
        out_shape=pltpu.VMEM((chips, CAP, width), jnp.bfloat16),
        in_specs=[vmem, vmem],
        out_specs=vmem,
        name="merge",
    )(in_vmem(keep), in_vmem(taken))
    returned = exchange(merged)
    expert_out = pl.pallas_call(
        combine_kernel,
        out_shape=jax.ShapeDtypeStruct(queries.shape, jnp.bfloat16),
        in_specs=[vmem, vmem],
        out_specs=vmem,
        name="combine",
    )(in_vmem(mix), in_vmem(returned))
    return attended, expert_out


def solution(mesh):
    rows = P(("dom", "exp"), None)
    return jax.shard_map(
        shards,
        mesh=mesh,
        in_specs=(
            rows,
            rows,
            rows,
            P(("dom", "exp"), None, None),
            P(("dom", "exp"), None, None),
            P(("dom", "exp")),
            P(),
            rows,
            rows,
            P("dom", None),
            P("exp", None),
            P("exp", None),
            P("exp", None),
        ),
        out_specs=(rows, rows),
        check_vma=False,
    )
```
